256 devices in a mesh: grp: 8 (over z_lo, core), dev: 32 (over x, y, z_hi).
Axes of the slice: x: 4, y: 4, z: 8 (z_hi: 2, z_lo: 4; z = z_hi * 4 + z_lo), core: 2. Of those that a mesh axis runs over, the one named last changes fastest.
Arguments:
- rollout: bfloat16 [256, 512, 1024], P('dev', 'grp'), may hold values from -6 to 6
- agent_gain: float32 [1024], replicated, may hold values from 0.25 to 1.75
- time_gain: float32 [1024], replicated, may hold values from 0.25 to 1.75
- inner_gain: float32 [1024], replicated, may hold values from 0.25 to 1.75
- agent_pair: bfloat16 [2, 1024, 512], replicated
- agent_value: bfloat16 [1024, 512], replicated, may hold values from -0.1875 to 0.1875
- agent_out: bfloat16 [512, 1024], replicated, may hold values from -0.25 to 0.25
- time_pair: bfloat16 [2, 1024, 512], replicated
- time_value: bfloat16 [1024, 512], replicated, may hold values from -0.1875 to 0.1875
- time_out: bfloat16 [512, 1024], replicated, may hold values from -0.25 to 0.25
- expand_weight: bfloat16 [1024, 2048], P('dev'), may hold values from -0.1875 to 0.1875
- reduce_weight: bfloat16 [2048, 1024], P(None, 'dev'), may hold values from -0.125 to 0.125
- episode_start: int32 [512], P(('grp', 'dev')), may hold values from 0 to 255, as said below
Outputs:
- layer_out: bfloat16 [256, 512, 1024], P('dev', 'grp')
The draws below stay inside these ranges and needn't reach their ends.
Inputs may be any that keep to these rules, and one draw needn't show every extreme that they name: episode_start[a] is the first step of agent a's current episode; earlier steps belong to its previous episode.
All inputs are finite; a program needn't handle non-finite values.
Results may differ from the reference program's by a relative error of at most 0.017.
Values may be sent and summed in bfloat16 or wider, within the bound.
No kernel may reach another device: no remote copies, remote signals or barrier semaphores. Data moves between devices by JAX's collectives and lax.ppermute only.
A program may use at most 128 MiB of HBM per device.

```python
import math
import jax
import jax.numpy as jnp
from jax import lax

D = 1024
HDIM = 64
FF = 2048
HW = 512
STEPS = 256
AGENTS = 512


def paired_weights(key, spread):
    first_key, second_key = jax.random.split(key)
    base_draw = jnp.clip(jax.random.normal(first_key, (D, HW), jnp.float32), -4.0, 4.0)
    other_draw = jnp.clip(jax.random.normal(second_key, (D, HW), jnp.float32), -4.0, 4.0)
    scale_factor = spread / math.sqrt(D)
    partner = other_draw
    return jnp.stack([base_draw * scale_factor, partner * scale_factor]).astype(jnp.bfloat16)


def draw_agent_pair(key, part):
    key = jax.random.fold_in(key, 11)
    return paired_weights(key, 2.0)


def draw_time_pair(key, part):
    key = jax.random.fold_in(key, 13)
    return paired_weights(key, 2.0)


def draw_episode_start(key, part):
    key = jax.random.fold_in(key, 5)
    first_key, second_key, third_key = jax.random.split(key, 3)
    offsets = jax.random.randint(first_key, (AGENTS,), 0, STEPS, jnp.int32)
    chosen = jax.random.randint(second_key, (), 0, AGENTS, jnp.int32)
    offsets = offsets.at[chosen].set(STEPS - 1)
    partner = (chosen + 1 + jax.random.randint(third_key, (), 0, AGENTS - 1, jnp.int32)) % AGENTS
    return offsets.at[partner].set(0)


def shard_levels(rng, shape, pieces, low, top_value):
    factor_of = 1.0
    for position, shards_of in pieces:
        heights = jax.random.uniform(jax.random.fold_in(jax.random.fold_in(rng, 6), position), (shards_of,), jnp.float32, low / len(pieces), top_value / len(pieces))
        factor_of = factor_of * jnp.repeat(jnp.exp(heights), shape[position] // shards_of).reshape((-1,) + (1,) * (len(shape) - 1 - position))
    return factor_of


def normal_values(rng, shape, scale, reach, pieces=(), dtype=jnp.bfloat16):
    values = scale * jax.random.normal(rng, shape, jnp.float32)
    if pieces:
        values = values * shard_levels(rng, shape, pieces, -0.22, 0.18)
    return jnp.clip(values, -reach, reach).astype(dtype)


def setup_inputs(seed: int = 0) -> dict:
    arg_keys = jax.random.split(jax.random.key(seed), 14)
    rollout = normal_values(arg_keys[0], (STEPS, AGENTS, D), 1.0, 6.0, ((0, 32), (1, 8)))
    agent_gain = jnp.clip(1.0 + 0.15 * jax.random.normal(arg_keys[1], (D,), jnp.float32), 0.25, 1.75)
    time_gain = jnp.clip(1.0 + 0.15 * jax.random.normal(arg_keys[2], (D,), jnp.float32), 0.25, 1.75)
    inner_gain = jnp.clip(1.0 + 0.15 * jax.random.normal(arg_keys[3], (D,), jnp.float32), 0.25, 1.75)
    agent_pair = draw_agent_pair(jax.random.fold_in(arg_keys[13], 71), 0)
    agent_value = normal_values(arg_keys[5], (D, HW), D ** -0.5, 0.1875)
    agent_out = normal_values(arg_keys[6], (HW, D), HW ** -0.5, 0.25)
    time_pair = draw_time_pair(jax.random.fold_in(arg_keys[13], 71), 0)
    time_value = normal_values(arg_keys[8], (D, HW), D ** -0.5, 0.1875)
    time_out = normal_values(arg_keys[9], (HW, D), HW ** -0.5, 0.25)
    expand_weight = normal_values(arg_keys[10], (D, FF), D ** -0.5, 0.1875, ((0, 32),))
    reduce_weight = normal_values(arg_keys[11], (FF, D), FF ** -0.5, 0.125, ((1, 32),))
    episode_start = draw_episode_start(jax.random.fold_in(arg_keys[13], 71), 0)
    return dict(rollout=rollout, agent_gain=agent_gain, time_gain=time_gain, inner_gain=inner_gain, agent_pair=agent_pair, agent_value=agent_value, agent_out=agent_out, time_pair=time_pair, time_value=time_value, time_out=time_out, expand_weight=expand_weight, reduce_weight=reduce_weight, episode_start=episode_start)


def rms_scale(row_block, gain_vec):
    widened = row_block.astype(jnp.float32)
    inverse = lax.rsqrt(lax.optimization_barrier(jnp.mean(widened * widened, axis=-1, keepdims=True)) + 1e-05)
    return (widened * inverse * gain_vec).astype(jnp.bfloat16)

def linear(row_block, weight):
    row_shape = row_block.shape
    flat_rows = row_block.reshape(-1, row_shape[-1])
    product = jnp.dot(flat_rows, weight, preferred_element_type=jnp.float32)
    return product.reshape(row_shape[:-1] + (weight.shape[1],))

def agent_attend(queries, key_rows, values):
    step_count, query_count, span_width = queries.shape
    head_count = span_width // HDIM
    query_heads = queries.reshape(step_count, query_count, head_count, HDIM).astype(jnp.float32)
    key_heads = key_rows.reshape(step_count, key_rows.shape[1], head_count, HDIM).astype(jnp.float32)
    value_heads = values.reshape(step_count, values.shape[1], head_count, HDIM)
    scores = jnp.einsum('tihd,tjhd->thij', query_heads, key_heads) * HDIM ** (-0.5)
    peak_score = lax.optimization_barrier(jnp.max(scores, axis=-1, keepdims=True))
    exponent = jnp.exp(scores - peak_score)
    weight_sum = lax.optimization_barrier(jnp.sum(exponent, axis=-1))
    rounded = exponent.astype(jnp.bfloat16)
    weighted = jnp.einsum('thij,tjhd->tihd', rounded.astype(jnp.float32), value_heads.astype(jnp.float32))
    context = weighted / jnp.transpose(weight_sum, (0, 2, 1))[..., None]
    return context.reshape(step_count, query_count, span_width).astype(jnp.bfloat16)

def time_attend(queries, key_rows, values, offsets):
    step_count, agent_count, span_width = queries.shape
    head_count = span_width // HDIM
    query_heads = queries.reshape(step_count, agent_count, head_count, HDIM).astype(jnp.float32)
    key_heads = key_rows.reshape(step_count, agent_count, head_count, HDIM).astype(jnp.float32)
    value_heads = values.reshape(step_count, agent_count, head_count, HDIM).astype(jnp.float32)
    scores = jnp.einsum('iahd,jahd->ahij', query_heads, key_heads) * HDIM ** (-0.5)
    places = lax.iota(jnp.int32, step_count)
    causal = places[:, None] >= places[None, :]
    begins = offsets[:, None, None]
    visible = causal[None] & ((places[None, None, :] >= begins) | (places[None, :, None] < begins))
    visible = visible[:, None]
    masked = jnp.where(visible, scores, -1e+30)
    peak_score = lax.optimization_barrier(jnp.max(masked, axis=-1, keepdims=True))
    exponent = jnp.where(visible, jnp.exp(masked - peak_score), 0.0)
    weight_sum = lax.optimization_barrier(jnp.sum(exponent, axis=-1))
    rounded = exponent.astype(jnp.bfloat16)
    weighted = jnp.einsum('ahij,jahd->iahd', rounded.astype(jnp.float32), value_heads)
    context = weighted / jnp.transpose(weight_sum, (2, 0, 1))[..., None]
    return context.reshape(step_count, agent_count, span_width).astype(jnp.bfloat16)

def reference(rollout, agent_gain, time_gain, inner_gain, agent_pair, agent_value, agent_out, time_pair, time_value, time_out, expand_weight, reduce_weight, episode_start):
    normed = rms_scale(rollout, agent_gain)
    queries = linear(normed, agent_pair[0]).astype(jnp.bfloat16)
    key_rows = linear(normed, agent_pair[1]).astype(jnp.bfloat16)
    values = linear(normed, agent_value).astype(jnp.bfloat16)

    def one_step(block_items):
        return agent_attend(block_items[0][None], block_items[1][None], block_items[2][None])[0]
    context = lax.map(one_step, (queries, key_rows, values))
    after_agents = (rollout.astype(jnp.float32) + linear(context, agent_out)).astype(jnp.bfloat16)
    normed_time = rms_scale(after_agents, time_gain)
    time_queries = jnp.swapaxes(linear(normed_time, time_pair[0]).astype(jnp.bfloat16), 0, 1)
    time_keys = jnp.swapaxes(linear(normed_time, time_pair[1]).astype(jnp.bfloat16), 0, 1)
    time_values = jnp.swapaxes(linear(normed_time, time_value).astype(jnp.bfloat16), 0, 1)

    def one_agent(block_items):
        return time_attend(block_items[0][:, None], block_items[1][:, None], block_items[2][:, None], block_items[3][None])[:, 0]
    time_context = jnp.swapaxes(lax.map(one_agent, (time_queries, time_keys, time_values, episode_start)), 0, 1)
    after_time = (after_agents.astype(jnp.float32) + linear(time_context, time_out)).astype(jnp.bfloat16)
    flat_rows = after_time.reshape(-1, after_time.shape[-1])
    inner_rows = rms_scale(flat_rows, inner_gain)
    hidden = jax.nn.gelu(jnp.dot(inner_rows, expand_weight, preferred_element_type=jnp.float32), approximate=True).astype(jnp.bfloat16)
    result = flat_rows.astype(jnp.float32) + jnp.dot(hidden, reduce_weight, preferred_element_type=jnp.float32)
    return result.astype(jnp.bfloat16).reshape(after_time.shape)
```

```python
import jax
import jax.numpy as jnp
from jax import lax
from jax.sharding import Mesh, PartitionSpec as P

HDIM = 64
GRP = ("zl", "c")
DEV = ("x", "y", "h")
BF = jnp.bfloat16
F32 = jnp.float32


def rms_scale(row_block, gain_vec):
    widened = row_block.astype(F32)
    inverse = lax.rsqrt(jnp.mean(widened * widened, axis=-1, keepdims=True) + 1e-05)
    return (widened * inverse * gain_vec).astype(BF)


def linear(rows, weight):
    return jnp.dot(rows, weight, preferred_element_type=F32)


def agent_attend(queries, key_rows, values):
    count, width = queries.shape
    heads = width // HDIM
    q = queries.reshape(count, heads, HDIM)
    k = key_rows.reshape(count, heads, HDIM)
    v = values.reshape(count, heads, HDIM)
    scores = jnp.einsum("ihd,jhd->hij", q, k, preferred_element_type=F32) * HDIM ** (-0.5)
    exponent = jnp.exp(scores - jnp.max(scores, axis=-1, keepdims=True))
    total = jnp.sum(exponent, axis=-1)
    weighted = jnp.einsum("hij,jhd->ihd", exponent.astype(BF), v, preferred_element_type=F32)
    context = weighted / jnp.transpose(total)[..., None]
    return context.reshape(count, width).astype(BF)


def time_attend(queries, key_rows, values, offsets, places):
    agents, steps, width = queries.shape
    heads = width // HDIM
    q = queries.reshape(agents, steps, heads, HDIM)
    k = key_rows.reshape(agents, steps, heads, HDIM)
    v = values.reshape(agents, steps, heads, HDIM)
    scores = jnp.einsum("aihd,ajhd->ahij", q, k, preferred_element_type=F32) * HDIM ** (-0.5)
    causal = places[:, None] >= places[None, :]
    begins = offsets[:, None, None]
    visible = causal[None] & ((places[None, None, :] >= begins) | (places[None, :, None] < begins))
    visible = visible[:, None]
    masked = jnp.where(visible, scores, -1e30)
    exponent = jnp.where(visible, jnp.exp(masked - jnp.max(masked, axis=-1, keepdims=True)), 0.0)
    total = jnp.sum(exponent, axis=-1)
    weighted = jnp.einsum("ahij,ajhd->aihd", exponent.astype(BF), v, preferred_element_type=F32)
    context = weighted / jnp.transpose(total, (0, 2, 1))[..., None]
    return context.reshape(agents, steps, width).astype(BF)


def on_device(
    rollout,
    agent_gain,
    time_gain,
    inner_gain,
    agent_pair,
    agent_value,
    agent_out,
    time_pair,
    time_value,
    time_out,
    expand_weight,
    reduce_weight,
    episode_start,
):
    steps_here, agents_here, width = rollout.shape
    n_grp = lax.axis_size(GRP)
    n_dev = lax.axis_size(DEV)
    agents_own = episode_start.shape[0]

    core, high = lax.axis_index("c"), lax.axis_index("h")
    half = expand_weight.shape[1] // 2
    up = lax.dynamic_slice_in_dim(expand_weight, core * half, half, 1)
    down = lax.dynamic_slice_in_dim(reduce_weight.T, core * half, half, 1)
    mine = jnp.stack([up, down])
    other = lax.ppermute(mine, "h", [(0, 1), (1, 0)])
    pair = jnp.where(
        high == 0, jnp.concatenate([mine, other], 1), jnp.concatenate([other, mine], 1)
    )
    near = lax.all_gather(pair, ("x", "y"), axis=1, tiled=True)
    far = lax.ppermute(near, "c", [(0, 1), (1, 0)])

    rows = lax.all_to_all(rollout, GRP, split_axis=0, concat_axis=0, tiled=True)
    rows = rows.reshape(n_grp * agents_here, width)
    normed = rms_scale(rows, agent_gain)
    queries = linear(normed, agent_pair[0]).astype(BF)
    key_rows = linear(normed, agent_pair[1]).astype(BF)
    values = linear(normed, agent_value).astype(BF)
    context = agent_attend(queries, key_rows, values)
    after_agents = (rows.astype(F32) + linear(context, agent_out)).astype(BF)

    pieces = after_agents.reshape(n_grp * n_dev, agents_own, width)
    series = lax.all_to_all(pieces, GRP + DEV, split_axis=0, concat_axis=0, tiled=True)
    series = jnp.swapaxes(series, 0, 1)
    steps = n_grp * n_dev
    index = lax.iota(jnp.int32, steps)
    places = (index % n_dev) * n_grp + index // n_dev
    series = series.reshape(agents_own * steps, width)
    normed_time = rms_scale(series, time_gain)
    shape = (agents_own, steps, -1)
    time_queries = linear(normed_time, time_pair[0]).astype(BF).reshape(shape)
    time_keys = linear(normed_time, time_pair[1]).astype(BF).reshape(shape)
    time_values = linear(normed_time, time_value).astype(BF).reshape(shape)
    time_context = time_attend(time_queries, time_keys, time_values, episode_start, places)
    time_context = time_context.reshape(agents_own * steps, -1)
    after_time = (series.astype(F32) + linear(time_context, time_out)).astype(BF)

    inner = rms_scale(after_time, inner_gain)
    total = after_time.astype(F32)
    for part in (near, far):
        hidden = jax.nn.gelu(linear(inner, part[0]), approximate=True).astype(BF)
        total = total + lax.dot_general(
            hidden, part[1], (((1,), (1,)), ((), ())), preferred_element_type=F32
        )
    result = total.astype(BF).reshape(agents_own, n_grp, n_dev, width)
    result = jnp.transpose(result, (1, 2, 0, 3))
    result = lax.all_to_all(result, DEV, split_axis=1, concat_axis=1, tiled=True)
    return result.reshape(steps_here, agents_here, width)


def solution(mesh):
    fine = Mesh(mesh.devices.reshape(4, 2, 4, 4, 2), ("zl", "c", "x", "y", "h"))
    return jax.shard_map(
        on_device,
        mesh=fine,
        in_specs=(
            P(DEV, GRP, None),
            P(),
            P(),
            P(),
            P(),
            P(),
            P(),
            P(),
            P(),
            P(),
            P(DEV, None),
            P(None, DEV),
            P(GRP + DEV),
        ),
        out_specs=P(DEV, GRP, None),
        check_vma=False,
    )
```

```python
import jax
import jax.numpy as jnp
from jax import lax
from jax.sharding import Mesh, PartitionSpec as P

HDIM = 64
GRP = ("zl", "c")
DEV = ("x", "y", "h")
BF = jnp.bfloat16
F32 = jnp.float32


def rms_scale(row_block, gain_vec):
    widened = row_block.astype(F32)
    inverse = lax.rsqrt(jnp.mean(widened * widened, axis=-1, keepdims=True) + 1e-05)
    return (widened * inverse * gain_vec).astype(BF)


def linear(rows, weight):
    return jnp.dot(rows, weight, preferred_element_type=F32)


def split_heads(rows):
    return rows.reshape(rows.shape[0], -1, HDIM)


def attend(queries, keys, values, visible=None):
    scores = jnp.einsum("ihd,jhd->hij", queries, keys, preferred_element_type=F32)
    scores = scores * HDIM ** (-0.5)
    if visible is not None:
        scores = jnp.where(visible, scores, -jnp.inf)
    exponent = jnp.exp(scores - jnp.max(scores, axis=-1, keepdims=True))
    total = jnp.sum(exponent, axis=-1)
    weighted = jnp.einsum("hij,jhd->ihd", exponent.astype(BF), values, preferred_element_type=F32)
    context = weighted / jnp.transpose(total)[..., None]
    return context.reshape(queries.shape[0], -1).astype(BF)


def swap_core(block):
    return lax.ppermute(block, "c", [(0, 1), (1, 0)])


def swap_z(block, k):
    n = lax.axis_size("zl")
    return lax.ppermute(block, "zl", [(i, i ^ k) for i in range(n)])


def by_xor(block, index):
    count = block.shape[0]
    bits = count.bit_length() - 1
    for bit in range(bits):
        parts = block.reshape((count >> (bit + 1), 2, 1 << bit) + block.shape[1:])
        flip = (index >> bit) & 1 == 1
        low, high = parts[:, :1], parts[:, 1:]
        parts = jnp.concatenate([jnp.where(flip, high, low), jnp.where(flip, low, high)], 1)
        block = parts.reshape(block.shape)
    return block


def on_device(
    rollout,
    agent_gain,
    time_gain,
    inner_gain,
    agent_pair,
    agent_value,
    agent_out,
    time_pair,
    time_value,
    time_out,
    expand_weight,
    reduce_weight,
    episode_start,
):
    steps_here, agents_here, width = rollout.shape
    zl, core, high = lax.axis_index("zl"), lax.axis_index("c"), lax.axis_index("h")
    n_zl, n_core = lax.axis_size("zl"), lax.axis_size("c")

    half = expand_weight.shape[1] // 2
    up = lax.dynamic_slice_in_dim(expand_weight, core * half, half, 1)
    down = lax.dynamic_slice_in_dim(reduce_weight.T, core * half, half, 1)
    mine = jnp.stack([up, down])
    other = lax.ppermute(mine, "h", [(0, 1), (1, 0)])

    by_step = rollout.reshape(n_zl, n_core, agents_here, width)
    keep = lax.dynamic_index_in_dim(by_step, core, 1, keepdims=False)
    give = lax.dynamic_index_in_dim(by_step, 1 - core, 1, keepdims=False)
    both = jnp.stack([keep, swap_core(give)], 1).reshape(n_zl, n_core * agents_here, width)
    chunks = [lax.dynamic_index_in_dim(both, zl ^ k, 0, keepdims=False) for k in range(n_zl)]
    chunks = [chunks[0]] + [swap_z(chunks[k], k) for k in range(1, n_zl)]
    rows = jnp.concatenate(chunks, 0)

    pair = jnp.where(
        high == 0, jnp.concatenate([mine, other], 1), jnp.concatenate([other, mine], 1)
    )
    near = lax.all_gather(pair, ("x", "y"), axis=1, tiled=True)
    far = swap_core(near)

    normed = rms_scale(rows, agent_gain)
    queries = linear(normed, agent_pair[0]).astype(BF)
    keys = split_heads(linear(normed, agent_pair[1]).astype(BF))
    values = split_heads(linear(normed, agent_value).astype(BF))
    size = n_core * agents_here
    back = [None] * n_zl
    for k in reversed(range(n_zl)):
        part = attend(split_heads(queries[k * size : (k + 1) * size]), keys, values)
        back[k] = swap_z(part, k) if k else part
    back = jnp.stack(back).reshape(n_zl, n_core, agents_here, -1)
    own, others = back[:, 0], swap_core(back[:, 1])
    context = jnp.stack([own, others], 1).reshape(steps_here, agents_here, -1)
    context = jnp.swapaxes(by_xor(context, zl * n_core + core), 0, 1)
    residual = jnp.swapaxes(rollout, 0, 1).reshape(-1, width).astype(F32)
    context = context.reshape(agents_here * steps_here, -1)
    after_agents = (residual + linear(context, agent_out)).astype(BF)

    n_dev = lax.axis_size(DEV)
    agents_own = episode_start.shape[0]
    steps = n_dev * steps_here
    pieces = after_agents.reshape(n_dev, agents_own, steps_here, width)
    series = lax.all_to_all(pieces, DEV, split_axis=0, concat_axis=0, tiled=True)
    places = lax.iota(jnp.int32, steps)
    causal = places[:, None] >= places[None, :]
    results = []
    for agent in range(agents_own):
        row_block = series[:, agent].reshape(steps, width)
        begin = episode_start[agent]
        visible = causal & ((places[None, :] >= begin) | (places[:, None] < begin))
        normed_time = rms_scale(row_block, time_gain)
        q = split_heads(linear(normed_time, time_pair[0]).astype(BF))
        k = split_heads(linear(normed_time, time_pair[1]).astype(BF))
        v = split_heads(linear(normed_time, time_value).astype(BF))
        time_context = attend(q, k, v, visible[None])
        results.append((row_block.astype(F32) + linear(time_context, time_out)).astype(BF))
    after_time = jnp.concatenate(results, 0)

    inner = rms_scale(after_time, inner_gain)
    total = after_time.astype(F32)
    for part in (near, far):
        hidden = jax.nn.gelu(linear(inner, part[0]), approximate=True).astype(BF)
        total = total + lax.dot_general(
            hidden, part[1], (((1,), (1,)), ((), ())), preferred_element_type=F32
        )
    result = total.astype(BF).reshape(agents_own, n_dev, steps_here, width)
    result = lax.all_to_all(
        jnp.swapaxes(result, 0, 1), DEV, split_axis=0, concat_axis=0, tiled=True
    )
    return jnp.swapaxes(result.reshape(agents_here, steps_here, width), 0, 1)


def solution(mesh):
    fine = Mesh(mesh.devices.reshape(4, 2, 4, 4, 2), ("zl", "c", "x", "y", "h"))
    return jax.shard_map(
        on_device,
        mesh=fine,
        in_specs=(
            P(DEV, GRP, None),
            P(),
            P(),
            P(),
            P(),
            P(),
            P(),
            P(),
            P(),
            P(),
            P(DEV, None),
            P(None, DEV),
            P(GRP + DEV),
        ),
        out_specs=P(DEV, GRP, None),
        check_vma=False,
    )
```

```python
import jax
import jax.numpy as jnp
from jax import lax
from jax.experimental import pallas as pl
from jax.experimental.pallas import tpu as pltpu
from jax.sharding import Mesh, PartitionSpec as P

HDIM = 64
GRP = ("zl", "c")
DEV = ("x", "y", "h")
BF = jnp.bfloat16
F32 = jnp.float32


def rms_scale(row_block, gain_vec):
    widened = row_block.astype(F32)
    inverse = lax.rsqrt(jnp.mean(widened * widened, axis=-1, keepdims=True) + 1e-05)
    return (widened * inverse * gain_vec).astype(BF)


def linear(rows, weight):
    return jnp.dot(rows, weight, preferred_element_type=F32)


def split_heads(rows):
    return rows.reshape(rows.shape[0], -1, HDIM)


def attend(queries, keys, values):
    scores = jnp.einsum("ihd,jhd->hij", queries, keys, preferred_element_type=F32)
    scores = scores * HDIM ** (-0.5)
    exponent = jnp.exp(scores - jnp.max(scores, axis=-1, keepdims=True))
    total = jnp.sum(exponent, axis=-1)
    weighted = jnp.einsum("hij,jhd->ihd", exponent.astype(BF), values, preferred_element_type=F32)
    context = weighted / jnp.transpose(total)[..., None]
    return context.reshape(queries.shape[0], -1).astype(BF)


LOG2E = 1.4426950408889634


def rms_block(rows, gain):
    inverse = lax.rsqrt(jnp.mean(rows * rows, axis=-1, keepdims=True) + 1e-05)
    return (rows * inverse * gain).astype(BF)


def time_kernel(start_ref, rows_ref, place_ref, place_row_ref, gain_ref, qk_ref, v_ref, o_ref, out_ref):
    agents, steps, width = rows_ref.shape
    later, earlier = place_ref[...], place_row_ref[...]
    for agent in range(agents):
        rows = rows_ref[agent].astype(F32)
        normed = rms_block(rows, gain_ref[...])
        queries = linear(normed, qk_ref[0]).astype(BF)
        keys = linear(normed, qk_ref[1]).astype(BF)
        values = linear(normed, v_ref[...]).astype(BF)
        begin = start_ref[agent]
        visible = (later >= earlier) & ((earlier >= begin) | (later < begin))
        context = []
        for h in range(queries.shape[1] // HDIM):
            part = slice(h * HDIM, (h + 1) * HDIM)
            scores = lax.dot_general(
                queries[:, part], keys[:, part], (((1,), (1,)), ((), ())), preferred_element_type=F32
            )
            scores = jnp.where(visible, scores, -jnp.inf)
            top = jnp.max(scores, axis=-1, keepdims=True)
            exponent = jnp.exp2((scores - top) * (LOG2E * HDIM ** (-0.5)))
            total = jnp.sum(exponent, axis=-1, keepdims=True)
            weighted = linear(exponent.astype(BF), values[:, part])
            context.append((weighted / total).astype(BF))
        context = jnp.concatenate(context, 1)
        out_ref[agent] = (rows + linear(context, o_ref[...])).astype(BF)


def time_block(series, places, starts, gain, pair, value, out):
    agents, steps, width = series.shape
    vmem = pl.BlockSpec(memory_space=pltpu.VMEM)
    return pl.pallas_call(
        time_kernel,
        out_shape=jax.ShapeDtypeStruct(series.shape, BF),
        in_specs=[pl.BlockSpec(memory_space=pltpu.SMEM)] + [vmem] * 7,
        out_specs=vmem,
        compiler_params=pltpu.CompilerParams(vmem_limit_bytes=28 << 20),
        cost_estimate=pl.CostEstimate(flops=3 << 30, bytes_accessed=6 << 20, transcendentals=1 << 20),
        name="time_attention",
    )(starts, series, places[:, None], places[None, :], gain[None, :], pair, value, out)


def gelu(x):
    inner = 0.7978845608028654 * (x + 0.044715 * (x * x * x))
    return (0.5 * x) * (1.0 + jnp.tanh(inner))


def ff_kernel(rows_ref, gain_ref, up_ref, down_ref, out_ref, inner, total):
    step, last = pl.program_id(0), pl.num_programs(0) - 1

    @pl.when(step == 0)
    def _():
        rows = rows_ref[...].astype(F32)
        inner[...] = rms_block(rows, gain_ref[...])
        total[...] = rows

    hidden = gelu(linear(inner[...], up_ref[0, 0])).astype(BF)
    total[...] += lax.dot_general(
        hidden, down_ref[0, 0], (((1,), (1,)), ((), ())), preferred_element_type=F32
    )

    @pl.when(step == last)
    def _():
        out_ref[...] = total[...].astype(BF)


def ff_block(rows, gain, weights):
    count, width = rows.shape
    halves, half = weights.shape[1], weights.shape[3]
    size = 512
    n = half // size
    whole = pl.BlockSpec((count, width), lambda i: (0, 0))
    up = pl.BlockSpec((1, 1, width, size), lambda i: (0, i // n, 0, i % n))
    down = pl.BlockSpec((1, 1, width, size), lambda i: (1, i // n, 0, i % n))
    return pl.pallas_call(
        ff_kernel,
        grid=(halves * n,),
        out_shape=jax.ShapeDtypeStruct((count, width), BF),
        in_specs=[whole, pl.BlockSpec((1, width), lambda i: (0, 0)), up, down],
        out_specs=whole,
        scratch_shapes=[pltpu.VMEM((count, width), BF), pltpu.VMEM((count, width), F32)],
        compiler_params=pltpu.CompilerParams(vmem_limit_bytes=28 << 20),
        cost_estimate=pl.CostEstimate(flops=4 << 30, bytes_accessed=10 << 20, transcendentals=1 << 20),
        name="feed_forward",
    )(rows, gain[None, :], weights, weights)


def swap_core(block):
    return lax.ppermute(block, "c", [(0, 1), (1, 0)])


def swap_z(block, k):
    n = lax.axis_size("zl")
    return lax.ppermute(block, "zl", [(i, i ^ k) for i in range(n)])


def other_half(block, zl, high):
    n = lax.axis_size("zl")
    spot = lambda h, z: z * 2 + h
    edge = [(spot(h, z), spot(1 - h, n - 1 - z)) for h in (0, 1) for z in (0, n - 1)]
    inner = [(spot(h, z), spot(h, w)) for h in (0, 1) for z, w in ((0, 1), (n - 1, n - 2))]
    outer = lax.ppermute(block, ("zl", "h"), edge)
    inward = lax.ppermute(outer, ("zl", "h"), inner)
    return jnp.where((zl == 0) | (zl == n - 1), outer, inward)


def on_device(
    rollout,
    agent_gain,
    time_gain,
    inner_gain,
    agent_pair,
    agent_value,
    agent_out,
    time_pair,
    time_value,
    time_out,
    expand_weight,
    reduce_weight,
    episode_start,
):
    steps_here, agents_here, width = rollout.shape
    zl, core, high = lax.axis_index("zl"), lax.axis_index("c"), lax.axis_index("h")
    n_zl, n_core = lax.axis_size("zl"), lax.axis_size("c")

    half = expand_weight.shape[1] // 2
    up = lax.dynamic_slice_in_dim(expand_weight, core * half, half, 1)
    down = lax.dynamic_slice_in_dim(reduce_weight.T, core * half, half, 1)
    mine = jnp.stack([up, down])
    other = other_half(mine, zl, high)

    by_step = rollout.reshape(n_zl, n_core, agents_here, width)
    chunks = [lax.dynamic_index_in_dim(by_step, zl ^ k, 0, keepdims=False) for k in range(n_zl)]
    chunks = [chunks[0]] + [swap_z(chunks[k], k) for k in range(1, n_zl)]
    keep = jnp.stack([lax.dynamic_index_in_dim(c, core, 0, keepdims=False) for c in chunks])
    give = jnp.stack([lax.dynamic_index_in_dim(c, 1 - core, 0, keepdims=False) for c in chunks])
    got = swap_core(give)
    both = jnp.stack([jnp.where(core == 0, keep, got), jnp.where(core == 0, got, keep)], 1)
    rows = jnp.zeros_like(both)
    for k in range(n_zl):
        rows = lax.dynamic_update_index_in_dim(rows, both[k], zl ^ k, 0)
    rows = rows.reshape(-1, width)

    rows, other = lax.optimization_barrier((rows, other))
    pair = jnp.where(
        high == 0, jnp.concatenate([mine, other], 1), jnp.concatenate([other, mine], 1)
    )
    weights = lax.all_gather(pair, ("c", "x", "y"), axis=1, tiled=True)
    weights = weights.reshape(2, n_core, width, half)

    normed = rms_scale(rows, agent_gain)
    queries = split_heads(linear(normed, agent_pair[0]).astype(BF))
    keys = split_heads(linear(normed, agent_pair[1]).astype(BF))
    values = split_heads(linear(normed, agent_value).astype(BF))
    context = attend(queries, keys, values)
    after_agents = (rows.astype(F32) + linear(context, agent_out)).astype(BF)

    n_grp, n_dev = n_zl * n_core, lax.axis_size(DEV)
    agents_own = episode_start.shape[0]
    steps = n_dev * steps_here
    pieces = after_agents.reshape(n_grp, n_dev, agents_own, width)
    pieces = jnp.swapaxes(pieces, 0, 1).reshape(steps, agents_own, width)
    series = lax.all_to_all(pieces, DEV + GRP, split_axis=0, concat_axis=0, tiled=True)
    series = jnp.swapaxes(series, 0, 1)
    places = lax.iota(jnp.int32, steps)
    after_time = time_block(
        series, places, episode_start, time_gain, time_pair, time_value, time_out
    )
    result = ff_block(after_time.reshape(-1, width), inner_gain, weights)
    result = result.reshape(agents_own, n_dev, steps_here, width)
    result = lax.all_to_all(
        jnp.swapaxes(result, 0, 1), DEV, split_axis=0, concat_axis=0, tiled=True
    )
    return jnp.swapaxes(result.reshape(agents_here, steps_here, width), 0, 1)


def solution(mesh):
    fine = Mesh(mesh.devices.reshape(4, 2, 4, 4, 2), ("zl", "c", "x", "y", "h"))
    return jax.shard_map(
        on_device,
        mesh=fine,
        in_specs=(
            P(DEV, GRP, None),
            P(),
            P(),
            P(),
            P(),
            P(),
            P(),
            P(),
            P(),
            P(),
            P(DEV, None),
            P(None, DEV),
            P(GRP + DEV),
        ),
        out_specs=P(DEV, GRP, None),
        check_vma=False,
    )
```

```python
import jax
import jax.numpy as jnp
from jax import lax
from jax.experimental import pallas as pl
from jax.experimental.pallas import tpu as pltpu
from jax.sharding import Mesh, PartitionSpec as P

HDIM = 64
GRP = ("zl", "c")
DEV = ("x", "y", "h")
TURNED = ("h", "x", "y")
BF = jnp.bfloat16
F32 = jnp.float32


def rms_scale(row_block, gain_vec):
    widened = row_block.astype(F32)
    inverse = lax.rsqrt(jnp.mean(widened * widened, axis=-1, keepdims=True) + 1e-05)
    return (widened * inverse * gain_vec).astype(BF)


def linear(rows, weight):
    return jnp.dot(rows, weight, preferred_element_type=F32)


def split_heads(rows):
    return rows.reshape(rows.shape[0], -1, HDIM)


def attend(queries, keys, values):
    scores = jnp.einsum("ihd,jhd->hij", queries, keys, preferred_element_type=F32)
    scores = scores * HDIM ** (-0.5)
    exponent = jnp.exp(scores - jnp.max(scores, axis=-1, keepdims=True))
    total = jnp.sum(exponent, axis=-1)
    weighted = jnp.einsum("hij,jhd->ihd", exponent.astype(BF), values, preferred_element_type=F32)
    context = weighted / jnp.transpose(total)[..., None]
    return context.reshape(queries.shape[0], -1).astype(BF)


LOG2E = 1.4426950408889634


def rms_block(rows, gain):
    inverse = lax.rsqrt(jnp.mean(rows * rows, axis=-1, keepdims=True) + 1e-05)
    return (rows * inverse * gain).astype(BF)


def time_kernel(start_ref, rows_ref, place_ref, place_row_ref, gain_ref, qk_ref, v_ref, o_ref, out_ref):
    agents, steps, width = rows_ref.shape
    later, earlier = place_ref[...], place_row_ref[...]
    for agent in range(agents):
        rows = rows_ref[agent].astype(F32)
        normed = rms_block(rows, gain_ref[...])
        queries = linear(normed, qk_ref[0]).astype(BF)
        keys = linear(normed, qk_ref[1]).astype(BF)
        values = linear(normed, v_ref[...]).astype(BF)
        begin = start_ref[agent]
        visible = (later >= earlier) & ((earlier >= begin) | (later < begin))
        context = []
        for h in range(queries.shape[1] // HDIM):
            part = slice(h * HDIM, (h + 1) * HDIM)
            scores = lax.dot_general(
                queries[:, part], keys[:, part], (((1,), (1,)), ((), ())), preferred_element_type=F32
            )
            scores = jnp.where(visible, scores, -jnp.inf)
            top = jnp.max(scores, axis=-1, keepdims=True)
            exponent = jnp.exp2((scores - top) * (LOG2E * HDIM ** (-0.5)))
            total = jnp.sum(exponent, axis=-1, keepdims=True)
            weighted = linear(exponent.astype(BF), values[:, part])
            context.append((weighted / total).astype(BF))
        context = jnp.concatenate(context, 1)
        out_ref[agent] = (rows + linear(context, o_ref[...])).astype(BF)


def time_block(series, places, starts, gain, pair, value, out):
    agents, steps, width = series.shape
    vmem = pl.BlockSpec(memory_space=pltpu.VMEM)
    return pl.pallas_call(
        time_kernel,
        out_shape=jax.ShapeDtypeStruct(series.shape, BF),
        in_specs=[pl.BlockSpec(memory_space=pltpu.SMEM)] + [vmem] * 7,
        out_specs=vmem,
        compiler_params=pltpu.CompilerParams(vmem_limit_bytes=28 << 20),
        cost_estimate=pl.CostEstimate(flops=3 << 30, bytes_accessed=6 << 20, transcendentals=1 << 20),
        name="time_attention",
    )(starts, series, places[:, None], places[None, :], gain[None, :], pair, value, out)


def gelu(x):
    inner = 0.7978845608028654 * (x + 0.044715 * (x * x * x))
    return (0.5 * x) * (1.0 + jnp.tanh(inner))


def ff_kernel(rows_ref, gain_ref, up_ref, down_ref, out_ref, inner, total):
    step, last = pl.program_id(0), pl.num_programs(0) - 1

    @pl.when(step == 0)
    def _():
        rows = rows_ref[...].astype(F32)
        inner[...] = rms_block(rows, gain_ref[...])
        total[...] = rows

    hidden = gelu(linear(inner[...], up_ref[0, 0])).astype(BF)
    total[...] += lax.dot_general(
        hidden, down_ref[0, 0], (((1,), (1,)), ((), ())), preferred_element_type=F32
    )

    @pl.when(step == last)
    def _():
        out_ref[...] = total[...].astype(BF)


def ff_block(rows, gain, weights):
    count, width = rows.shape
    halves, half = weights.shape[1], weights.shape[3]
    size = 512
    n = half // size
    whole = pl.BlockSpec((count, width), lambda i: (0, 0))
    up = pl.BlockSpec((1, 1, width, size), lambda i: (0, i // n, 0, i % n))
    down = pl.BlockSpec((1, 1, width, size), lambda i: (1, i // n, 0, i % n))
    return pl.pallas_call(
        ff_kernel,
        grid=(halves * n,),
        out_shape=jax.ShapeDtypeStruct((count, width), BF),
        in_specs=[whole, pl.BlockSpec((1, width), lambda i: (0, 0)), up, down],
        out_specs=whole,
        scratch_shapes=[pltpu.VMEM((count, width), BF), pltpu.VMEM((count, width), F32)],
        compiler_params=pltpu.CompilerParams(vmem_limit_bytes=58 << 20),
        cost_estimate=pl.CostEstimate(flops=4 << 30, bytes_accessed=10 << 20, transcendentals=1 << 20),
        name="feed_forward",
    )(rows, gain[None, :], weights, weights)


def swap_core(block):
    return lax.ppermute(block, "c", [(0, 1), (1, 0)])


def swap_z(block, k):
    n = lax.axis_size("zl")
    return lax.ppermute(block, "zl", [(i, i ^ k) for i in range(n)])


def other_half(block, zl, high):
    n = lax.axis_size("zl")
    spot = lambda h, z: z * 2 + h
    edge = [(spot(h, z), spot(1 - h, n - 1 - z)) for h in (0, 1) for z in (0, n - 1)]
    inner = [(spot(h, z), spot(h, w)) for h in (0, 1) for z, w in ((0, 1), (n - 1, n - 2))]
    outer = lax.ppermute(block, ("zl", "h"), edge)
    inward = lax.ppermute(outer, ("zl", "h"), inner)
    return jnp.where((zl == 0) | (zl == n - 1), outer, inward)


def on_device(
    rollout,
    agent_gain,
    time_gain,
    inner_gain,
    agent_pair,
    agent_value,
    agent_out,
    time_pair,
    time_value,
    time_out,
    expand_weight,
    reduce_weight,
    episode_start,
):
    steps_here, agents_here, width = rollout.shape
    zl, core, high = lax.axis_index("zl"), lax.axis_index("c"), lax.axis_index("h")
    n_zl, n_core = lax.axis_size("zl"), lax.axis_size("c")

    half = expand_weight.shape[1] // 2
    up = lax.dynamic_slice_in_dim(expand_weight, core * half, half, 1)
    down = lax.dynamic_slice_in_dim(reduce_weight.T, core * half, half, 1)
    mine = jnp.stack([up, down])
    other = other_half(mine, zl, high)

    by_step = rollout.reshape(n_zl, n_core, agents_here, width)
    chunks = [lax.dynamic_index_in_dim(by_step, zl ^ k, 0, keepdims=False) for k in range(n_zl)]
    arrived = [swap_z(chunks[k], k) for k in range(1, n_zl)]
    arrived, other = lax.optimization_barrier((arrived, other))
    chunks = chunks[:1] + arrived
    keep = jnp.stack([lax.dynamic_index_in_dim(c, core, 0, keepdims=False) for c in chunks])
    give = jnp.stack([lax.dynamic_index_in_dim(c, 1 - core, 0, keepdims=False) for c in chunks])
    got = swap_core(give)
    both = jnp.stack([jnp.where(core == 0, keep, got), jnp.where(core == 0, got, keep)], 1)
    rows = jnp.zeros_like(both)
    for k in range(n_zl):
        rows = lax.dynamic_update_index_in_dim(rows, both[k], zl ^ k, 0)
    rows = rows.reshape(-1, width)

    pair = jnp.where(
        high == 0, jnp.concatenate([mine, other], 1), jnp.concatenate([other, mine], 1)
    )
    weights = lax.all_gather(pair, ("c", "x", "y"), axis=1, tiled=True)
    weights = weights.reshape(2, n_core, width, half)

    normed = rms_scale(rows, agent_gain)
    queries = split_heads(linear(normed, agent_pair[0]).astype(BF))
    keys = split_heads(linear(normed, agent_pair[1]).astype(BF))
    values = split_heads(linear(normed, agent_value).astype(BF))
    context = attend(queries, keys, values)
    after_agents = (rows.astype(F32) + linear(context, agent_out)).astype(BF)

    n_grp, n_dev = n_zl * n_core, lax.axis_size(DEV)
    agents_own = episode_start.shape[0]
    steps = n_dev * steps_here
    n_high = lax.axis_size("h")
    n_flat = n_dev // n_high
    pieces = after_agents.reshape(n_grp, n_flat, n_high, agents_own, width)
    pieces = jnp.transpose(pieces, (2, 1, 0, 3, 4)).reshape(steps, agents_own, width)
    series = lax.all_to_all(pieces, TURNED + GRP, split_axis=0, concat_axis=0, tiled=True)
    series = jnp.swapaxes(series, 0, 1)
    places = lax.iota(jnp.int32, steps).reshape(n_flat, n_high, n_grp)
    places = jnp.swapaxes(places, 0, 1).reshape(steps)
    after_time = time_block(
        series, places, episode_start, time_gain, time_pair, time_value, time_out
    )
    result = ff_block(after_time.reshape(-1, width), inner_gain, weights)
    result = result.reshape(agents_own, n_dev, steps_here, width)
    result = lax.all_to_all(
        jnp.swapaxes(result, 0, 1), TURNED, split_axis=0, concat_axis=0, tiled=True
    )
    result = result.reshape(n_high, n_flat, agents_own, steps_here, width)
    return jnp.transpose(result, (3, 1, 0, 2, 4)).reshape(steps_here, agents_here, width)


def solution(mesh):
    fine = Mesh(mesh.devices.reshape(4, 2, 4, 4, 2), ("zl", "c", "x", "y", "h"))
    return jax.shard_map(
        on_device,
        mesh=fine,
        in_specs=(
            P(DEV, GRP, None),
            P(),
            P(),
            P(),
            P(),
            P(),
            P(),
            P(),
            P(),
            P(),
            P(DEV, None),
            P(None, DEV),
            P(GRP + DEV),
        ),
        out_specs=P(DEV, GRP, None),
        check_vma=False,
    )
```

```python
import jax
import jax.numpy as jnp
from jax import lax
from jax.experimental import pallas as pl
from jax.experimental.pallas import tpu as pltpu
from jax.sharding import Mesh, PartitionSpec as P

HDIM = 64
GRP = ("zl", "c")
DEV = ("x", "y", "h")
TURNED = ("h", "x", "y")
BF = jnp.bfloat16
F32 = jnp.float32


def rms_scale(row_block, gain_vec):
    widened = row_block.astype(F32)
    inverse = lax.rsqrt(jnp.mean(widened * widened, axis=-1, keepdims=True) + 1e-05)
    return (widened * inverse * gain_vec).astype(BF)


def linear(rows, weight):
    return jnp.dot(rows, weight, preferred_element_type=F32)


def split_heads(rows):
    return rows.reshape(rows.shape[0], -1, HDIM)


def attend(queries, keys, values):
    scores = jnp.einsum("ihd,jhd->hij", queries, keys, preferred_element_type=F32)
    scores = scores * HDIM ** (-0.5)
    exponent = jnp.exp(scores - jnp.max(scores, axis=-1, keepdims=True))
    total = jnp.sum(exponent, axis=-1)
    weighted = jnp.einsum("hij,jhd->ihd", exponent.astype(BF), values, preferred_element_type=F32)
    context = weighted / jnp.transpose(total)[..., None]
    return context.reshape(queries.shape[0], -1).astype(BF)


LOG2E = 1.4426950408889634


def rms_block(rows, gain):
    inverse = lax.rsqrt(jnp.mean(rows * rows, axis=-1, keepdims=True) + 1e-05)
    return (rows * inverse * gain).astype(BF)


def time_kernel(start_ref, rows_ref, place_ref, place_row_ref, gain_ref, qk_ref, v_ref, o_ref, out_ref):
    agents, steps, width = out_ref.shape
    later, earlier = place_ref[...], place_row_ref[...]
    for agent in range(agents):
        rows = rows_ref[:, agent].astype(F32).reshape(steps, width)
        normed = rms_block(rows, gain_ref[...])
        queries = linear(normed, qk_ref[0]).astype(BF)
        keys = linear(normed, qk_ref[1]).astype(BF)
        values = linear(normed, v_ref[...]).astype(BF)
        begin = start_ref[agent]
        visible = (later >= earlier) & ((earlier >= begin) | (later < begin))
        context = []
        for h in range(queries.shape[1] // HDIM):
            part = slice(h * HDIM, (h + 1) * HDIM)
            scores = lax.dot_general(
                queries[:, part], keys[:, part], (((1,), (1,)), ((), ())), preferred_element_type=F32
            )
            scores = jnp.where(visible, scores, -jnp.inf)
            top = jnp.max(scores, axis=-1, keepdims=True)
            exponent = jnp.exp2((scores - top) * (LOG2E * HDIM ** (-0.5)))
            total = jnp.sum(exponent, axis=-1, keepdims=True)
            weighted = linear(exponent.astype(BF), values[:, part])
            context.append((weighted / total).astype(BF))
        context = jnp.concatenate(context, 1)
        out_ref[agent] = (rows + linear(context, o_ref[...])).astype(BF)


def time_block(series, places, starts, gain, pair, value, out):
    blocks, agents, block, width = series.shape
    vmem = pl.BlockSpec(memory_space=pltpu.VMEM)
    return pl.pallas_call(
        time_kernel,
        out_shape=jax.ShapeDtypeStruct((agents, blocks * block, width), BF),
        in_specs=[pl.BlockSpec(memory_space=pltpu.SMEM)] + [vmem] * 7,
        out_specs=vmem,
        compiler_params=pltpu.CompilerParams(vmem_limit_bytes=28 << 20),
        cost_estimate=pl.CostEstimate(flops=3 << 30, bytes_accessed=6 << 20, transcendentals=1 << 20),
        name="time_attention",
    )(starts, series, places[:, None], places[None, :], gain[None, :], pair, value, out)


def gelu(x):
    inner = 0.7978845608028654 * (x + 0.044715 * (x * x * x))
    return (0.5 * x) * (1.0 + jnp.tanh(inner))


def ff_kernel(rows_ref, gain_ref, up_ref, down_ref, out_ref, inner, total):
    step, last = pl.program_id(0), pl.num_programs(0) - 1

    @pl.when(step == 0)
    def _():
        rows = rows_ref[...].astype(F32)
        inner[...] = rms_block(rows, gain_ref[...])
        total[...] = rows

    hidden = gelu(linear(inner[...], up_ref[0, 0])).astype(BF)
    total[...] += lax.dot_general(
        hidden, down_ref[0, 0], (((1,), (1,)), ((), ())), preferred_element_type=F32
    )

    @pl.when(step == last)
    def _():
        blocks, agents, block, width = out_ref.shape
        for agent in range(agents):
            part = total[agent * blocks * block : (agent + 1) * blocks * block]
            out_ref[:, agent] = part.reshape(blocks, block, width).astype(BF)


def ff_block(rows, gain, weights, shape):
    rows = rows.reshape(-1, rows.shape[-1])
    count, width = rows.shape
    halves, half = weights.shape[1], weights.shape[3]
    size = 512
    n = half // size
    whole = pl.BlockSpec((count, width), lambda i: (0, 0))
    up = pl.BlockSpec((1, 1, width, size), lambda i: (0, i // n, 0, i % n))
    down = pl.BlockSpec((1, 1, width, size), lambda i: (1, i // n, 0, i % n))
    return pl.pallas_call(
        ff_kernel,
        grid=(halves * n,),
        out_shape=jax.ShapeDtypeStruct(shape, BF),
        in_specs=[whole, pl.BlockSpec((1, width), lambda i: (0, 0)), up, down],
        out_specs=pl.BlockSpec(shape, lambda i: (0, 0, 0, 0)),
        scratch_shapes=[pltpu.VMEM((count, width), BF), pltpu.VMEM((count, width), F32)],
        compiler_params=pltpu.CompilerParams(vmem_limit_bytes=54 << 20),
        cost_estimate=pl.CostEstimate(flops=4 << 30, bytes_accessed=10 << 20, transcendentals=1 << 20),
        name="feed_forward",
    )(rows, gain[None, :], weights, weights)


def pick(places, rows):
    count = rows.shape[0]
    spot = lax.broadcasted_iota(jnp.int32, (places.shape[0], count), 1)
    return linear(jnp.where(spot == places, 1.0, 0.0).astype(BF), rows)


def home_kernel(rows_place, context_place, rows_ref, own0, own1, own2, own3, got_ref, o_ref, out_ref):
    width = rows_ref.shape[-1]
    owns = [own0, own1, own2, own3]
    half = own0.shape[0] // 2
    got = got_ref[...].reshape(-1, got_ref.shape[-1])
    context = jnp.concatenate([own[:half] for own in owns] + [got], 0)
    residual = pick(rows_place[...], rows_ref[...].reshape(-1, width))
    context = pick(context_place[...], context).astype(BF)
    after = residual + linear(context, o_ref[...])
    out_ref[...] = after.reshape(out_ref.shape).astype(BF)


def home_block(rows_place, context_place, rows, back, got, out, shape):
    vmem = pl.BlockSpec(memory_space=pltpu.VMEM)
    return pl.pallas_call(
        home_kernel,
        out_shape=jax.ShapeDtypeStruct(shape, BF),
        in_specs=[vmem] * 9,
        out_specs=vmem,
        compiler_params=pltpu.CompilerParams(vmem_limit_bytes=24 << 20),
        cost_estimate=pl.CostEstimate(flops=1 << 30, bytes_accessed=4 << 20, transcendentals=0),
        name="home",
    )(rows_place[:, None], context_place[:, None], rows, *back, got, out)


def reorder_kernel(place, rows_ref, out_ref):
    rows = rows_ref[...].astype(F32).reshape(-1, rows_ref.shape[-1]).astype(BF)
    out_ref[...] = pick(place[...], rows).astype(BF)


def reorder(place, rows):
    vmem = pl.BlockSpec(memory_space=pltpu.VMEM)
    return pl.pallas_call(
        reorder_kernel,
        out_shape=jax.ShapeDtypeStruct((place.shape[0], rows.shape[-1]), BF),
        in_specs=[vmem] * 2,
        out_specs=vmem,
        compiler_params=pltpu.CompilerParams(vmem_limit_bytes=16 << 20),
        cost_estimate=pl.CostEstimate(flops=1 << 29, bytes_accessed=2 << 20, transcendentals=0),
        name="reorder",
    )(place[:, None], rows)


def swap_core(block):
    return lax.ppermute(block, "c", [(0, 1), (1, 0)])


def swap_z(block, k):
    n = lax.axis_size("zl")
    return lax.ppermute(block, "zl", [(i, i ^ k) for i in range(n)])


def on_device(
    rollout,
    agent_gain,
    time_gain,
    inner_gain,
    agent_pair,
    agent_value,
    agent_out,
    time_pair,
    time_value,
    time_out,
    expand_weight,
    reduce_weight,
    episode_start,
):
    steps_here, agents_here, width = rollout.shape
    zl, core = lax.axis_index("zl"), lax.axis_index("c")
    n_zl, n_core = lax.axis_size("zl"), lax.axis_size("c")

    half = expand_weight.shape[1] // 2
    up = lax.dynamic_slice_in_dim(expand_weight, core * half, half, 1)
    down = lax.dynamic_slice_in_dim(reduce_weight.T, core * half, half, 1)
    mine = jnp.stack([up, down])
    pair = lax.all_gather(mine, "h", axis=1, tiled=True)

    by_step = rollout.reshape(n_zl, n_core, agents_here, width)
    chunks = [lax.dynamic_index_in_dim(by_step, zl ^ k, 0, keepdims=False) for k in range(n_zl)]
    arrived = [swap_z(chunks[k], k) for k in range(1, n_zl)]
    arrived, pair = lax.optimization_barrier((arrived, pair))
    chunks = chunks[:1] + arrived
    keep = jnp.stack([lax.dynamic_index_in_dim(c, core, 0, keepdims=False) for c in chunks])
    give = jnp.stack([lax.dynamic_index_in_dim(c, 1 - core, 0, keepdims=False) for c in chunks])
    got = swap_core(give)
    size = n_core * agents_here
    rows = jnp.stack([keep, got], 1).reshape(n_zl * size, width)

    weights = lax.all_gather(pair, ("c", "x", "y"), axis=1, tiled=True)
    weights = weights.reshape(2, n_core, width, half)

    normed = rms_scale(rows, agent_gain)
    queries = linear(normed, agent_pair[0]).astype(BF)
    keys = split_heads(linear(normed, agent_pair[1]).astype(BF))
    values = split_heads(linear(normed, agent_value).astype(BF))
    back = [None] * n_zl
    for k in reversed(range(n_zl)):
        part = attend(split_heads(queries[k * size : (k + 1) * size]), keys, values)
        back[k] = swap_z(part, k) if k else part
    got = swap_core(jnp.stack([block[agents_here:] for block in back]))

    n_dev, n_high = lax.axis_size(DEV), lax.axis_size("h")
    n_flat = n_dev // n_high
    agents_own = episode_start.shape[0]
    steps = n_dev * steps_here
    at_home = lax.iota(jnp.int32, steps_here * agents_here)
    turned = at_home.reshape(steps_here, n_flat, n_high, agents_own)
    turned = jnp.transpose(turned, (2, 1, 3, 0)).reshape(-1)
    agent, source = turned % agents_here, (turned // agents_here) ^ (zl * n_core + core)
    in_context = ((source % n_core) * n_zl + source // n_core) * agents_here + agent
    shape = (n_dev, agents_own, steps_here, width)
    pieces = home_block(turned, in_context, rollout, back, got, agent_out, shape)

    series = lax.all_to_all(pieces, TURNED, split_axis=0, concat_axis=0, tiled=True)
    places = lax.iota(jnp.int32, steps).reshape(n_flat, n_high, steps_here)
    places = jnp.swapaxes(places, 0, 1).reshape(steps)
    after_time = time_block(
        series, places, episode_start, time_gain, time_pair, time_value, time_out
    )
    result = ff_block(after_time, inner_gain, weights, series.shape)
    result = lax.all_to_all(result, TURNED, split_axis=0, concat_axis=0, tiled=True)
    back_home = at_home.reshape(n_high, n_flat, agents_own, steps_here)
    back_home = jnp.transpose(back_home, (3, 1, 0, 2)).reshape(-1)
    return reorder(back_home, result).reshape(steps_here, agents_here, width)


def solution(mesh):
    fine = Mesh(mesh.devices.reshape(4, 2, 4, 4, 2), ("zl", "c", "x", "y", "h"))
    return jax.shard_map(
        on_device,
        mesh=fine,
        in_specs=(
            P(DEV, GRP, None),
            P(),
            P(),
            P(),
            P(),
            P(),
            P(),
            P(),
            P(),
            P(),
            P(DEV, None),
            P(None, DEV),
            P(GRP + DEV),
        ),
        out_specs=P(DEV, GRP, None),
        check_vma=False,
    )
```

```python
import jax
import jax.numpy as jnp
from jax import lax
from jax.experimental import pallas as pl
from jax.experimental.pallas import tpu as pltpu
from jax.sharding import Mesh, PartitionSpec as P

HDIM = 64
GRP = ("zl", "c")
DEV = ("x", "y", "h")
TURNED = ("h", "x", "y")
BF = jnp.bfloat16
F32 = jnp.float32


def rms_scale(row_block, gain_vec):
    widened = row_block.astype(F32)
    inverse = lax.rsqrt(jnp.mean(widened * widened, axis=-1, keepdims=True) + 1e-05)
    return (widened * inverse * gain_vec).astype(BF)


def linear(rows, weight):
    return jnp.dot(rows, weight, preferred_element_type=F32)


def split_heads(rows):
    return rows.reshape(rows.shape[0], -1, HDIM)


def attend(queries, keys, values):
    scores = jnp.einsum("ihd,jhd->hij", queries, keys, preferred_element_type=F32)
    scores = scores * HDIM ** (-0.5)
    exponent = jnp.exp(scores - jnp.max(scores, axis=-1, keepdims=True))
    total = jnp.sum(exponent, axis=-1)
    weighted = jnp.einsum("hij,jhd->ihd", exponent.astype(BF), values, preferred_element_type=F32)
    context = weighted / jnp.transpose(total)[..., None]
    return context.reshape(queries.shape[0], -1).astype(BF)


LOG2E = 1.4426950408889634


def rms_block(rows, gain):
    inverse = lax.rsqrt(jnp.mean(rows * rows, axis=-1, keepdims=True) + 1e-05)
    return (rows * inverse * gain).astype(BF)


def time_kernel(start_ref, rows_ref, place_ref, place_row_ref, gain_ref, qk_ref, v_ref, o_ref, out_ref):
    agents, steps, width = rows_ref.shape
    later, earlier = place_ref[...], place_row_ref[...]
    for agent in range(agents):
        rows = rows_ref[agent].astype(F32)
        normed = rms_block(rows, gain_ref[...])
        queries = linear(normed, qk_ref[0]).astype(BF)
        keys = linear(normed, qk_ref[1]).astype(BF)
        values = linear(normed, v_ref[...]).astype(BF)
        begin = start_ref[agent]
        visible = (later >= earlier) & ((earlier >= begin) | (later < begin))
        context = []
        for h in range(queries.shape[1] // HDIM):
            part = slice(h * HDIM, (h + 1) * HDIM)
            scores = lax.dot_general(
                queries[:, part], keys[:, part], (((1,), (1,)), ((), ())), preferred_element_type=F32
            )
            scores = jnp.where(visible, scores, -jnp.inf)
            top = jnp.max(scores, axis=-1, keepdims=True)
            exponent = jnp.exp2((scores - top) * (LOG2E * HDIM ** (-0.5)))
            total = jnp.sum(exponent, axis=-1, keepdims=True)
            weighted = linear(exponent.astype(BF), values[:, part])
            context.append((weighted / total).astype(BF))
        context = jnp.concatenate(context, 1)
        out_ref[agent] = (rows + linear(context, o_ref[...])).astype(BF)


def time_block(series, places, starts, gain, pair, value, out):
    agents, steps, width = series.shape
    vmem = pl.BlockSpec(memory_space=pltpu.VMEM)
    return pl.pallas_call(
        time_kernel,
        out_shape=jax.ShapeDtypeStruct(series.shape, BF),
        in_specs=[pl.BlockSpec(memory_space=pltpu.SMEM)] + [vmem] * 7,
        out_specs=vmem,
        compiler_params=pltpu.CompilerParams(vmem_limit_bytes=28 << 20),
        cost_estimate=pl.CostEstimate(flops=3 << 30, bytes_accessed=6 << 20, transcendentals=1 << 20),
        name="time_attention",
    )(starts, series, places[:, None], places[None, :], gain[None, :], pair, value, out)


def gelu(x):
    inner = 0.7978845608028654 * (x + 0.044715 * (x * x * x))
    return (0.5 * x) * (1.0 + jnp.tanh(inner))


def ff_kernel(rows_ref, gain_ref, weights_ref, out_ref, held, arrived):
    halves, width, half = weights_ref.shape[1:]
    size = half // 2
    parts = [(i, j) for i in range(halves) for j in range(half // size)]

    def fetch(n, which):
        i, j = parts[n]
        source = weights_ref.at[which, i, :, pl.ds(j * size, size)]
        return pltpu.make_async_copy(source, held.at[n, which], arrived.at[n, which])

    for n in range(len(parts)):
        fetch(n, 0).start()
        fetch(n, 1).start()
    total = rows_ref[...].astype(F32)
    inner = rms_block(total, gain_ref[...])
    for n in range(len(parts)):
        fetch(n, 0).wait()
        hidden = gelu(linear(inner, held[n, 0])).astype(BF)
        fetch(n, 1).wait()
        total = total + lax.dot_general(
            hidden, held[n, 1], (((1,), (1,)), ((), ())), preferred_element_type=F32
        )
    blocks, agents, block, _ = out_ref.shape
    for agent in range(agents):
        part = total[agent * blocks * block : (agent + 1) * blocks * block]
        out_ref[:, agent] = part.reshape(blocks, block, width).astype(BF)


def ff_block(rows, gain, weights, shape):
    halves, width, half = weights.shape[1:]
    size = half // 2
    vmem = pl.BlockSpec(memory_space=pltpu.VMEM)
    return pl.pallas_call(
        ff_kernel,
        out_shape=jax.ShapeDtypeStruct(shape, BF),
        in_specs=[vmem, vmem, pl.BlockSpec(memory_space=pltpu.HBM)],
        out_specs=vmem,
        scratch_shapes=[
            pltpu.VMEM((2 * halves, 2, width, size), BF),
            pltpu.SemaphoreType.DMA((2 * halves, 2)),
        ],
        compiler_params=pltpu.CompilerParams(vmem_limit_bytes=53 << 20),
        cost_estimate=pl.CostEstimate(flops=4 << 30, bytes_accessed=10 << 20, transcendentals=1 << 20),
        name="feed_forward",
    )(rows, gain[None, :], weights)


def pick(places, rows):
    count = rows.shape[0]
    spot = lax.broadcasted_iota(jnp.int32, (places.shape[0], count), 1)
    return linear(jnp.where(spot == places, 1.0, 0.0).astype(BF), rows)


def reorder_kernel(place, rows_ref, out_ref):
    rows = rows_ref[...].astype(F32).reshape(-1, rows_ref.shape[-1]).astype(BF)
    out_ref[...] = pick(place[...], rows).astype(BF)


def reorder(place, rows):
    vmem = pl.BlockSpec(memory_space=pltpu.VMEM)
    return pl.pallas_call(
        reorder_kernel,
        out_shape=jax.ShapeDtypeStruct((place.shape[0], rows.shape[-1]), BF),
        in_specs=[vmem] * 2,
        out_specs=vmem,
        compiler_params=pltpu.CompilerParams(vmem_limit_bytes=16 << 20),
        cost_estimate=pl.CostEstimate(flops=1 << 29, bytes_accessed=2 << 20, transcendentals=0),
        name="reorder",
    )(place[:, None], rows)


def on_device(
    rollout,
    agent_gain,
    time_gain,
    inner_gain,
    agent_pair,
    agent_value,
    agent_out,
    time_pair,
    time_value,
    time_out,
    expand_weight,
    reduce_weight,
    episode_start,
):
    steps_here, agents_here, width = rollout.shape
    core, high = lax.axis_index("c"), lax.axis_index("h")
    n_grp, n_core = lax.axis_size(GRP), lax.axis_size("c")

    half = expand_weight.shape[1] // 2
    up = lax.dynamic_slice_in_dim(expand_weight, core * half, half, 1)
    down = lax.dynamic_slice_in_dim(reduce_weight.T, core * half, half, 1)
    mine = jnp.stack([up, down])
    rollout, mine = lax.optimization_barrier((rollout, mine))
    other = lax.ppermute(mine, "h", [(0, 1), (1, 0)])

    rows = lax.all_to_all(rollout, GRP, split_axis=0, concat_axis=0, tiled=True)
    rows = rows.reshape(n_grp * agents_here, width)
    rows, other = lax.optimization_barrier((rows, other))

    pair = jnp.where(
        high == 0, jnp.concatenate([mine, other], 1), jnp.concatenate([other, mine], 1)
    )
    weights = lax.all_gather(pair, ("c", "x", "y"), axis=1, tiled=True)
    weights = weights.reshape(2, n_core, width, half)

    normed = rms_scale(rows, agent_gain)
    queries = split_heads(linear(normed, agent_pair[0]).astype(BF))
    keys = split_heads(linear(normed, agent_pair[1]).astype(BF))
    values = split_heads(linear(normed, agent_value).astype(BF))
    context = attend(queries, keys, values)
    after_agents = (rows.astype(F32) + linear(context, agent_out)).astype(BF)

    n_dev = lax.axis_size(DEV)
    agents_own = episode_start.shape[0]
    steps = n_dev * steps_here
    n_high = lax.axis_size("h")
    n_flat = n_dev // n_high
    pieces = after_agents.reshape(n_grp, n_flat, n_high, agents_own, width)
    pieces = jnp.transpose(pieces, (2, 1, 0, 3, 4)).reshape(steps, agents_own, width)
    series = lax.all_to_all(pieces, TURNED + GRP, split_axis=0, concat_axis=0, tiled=True)
    series = jnp.swapaxes(series, 0, 1)
    places = lax.iota(jnp.int32, steps).reshape(n_flat, n_high, n_grp)
    places = jnp.swapaxes(places, 0, 1).reshape(steps)
    after_time = time_block(
        series, places, episode_start, time_gain, time_pair, time_value, time_out
    )
    shape = (n_dev, agents_own, steps_here, width)
    result = ff_block(after_time.reshape(-1, width), inner_gain, weights, shape)
    result = lax.all_to_all(result, TURNED, split_axis=0, concat_axis=0, tiled=True)
    order = lax.iota(jnp.int32, steps_here * agents_here)
    order = order.reshape(n_high, n_flat, agents_own, steps_here)
    order = jnp.transpose(order, (3, 1, 0, 2)).reshape(-1)
    return reorder(order, result).reshape(steps_here, agents_here, width)


def solution(mesh):
    fine = Mesh(mesh.devices.reshape(4, 2, 4, 4, 2), ("zl", "c", "x", "y", "h"))
    return jax.shard_map(
        on_device,
        mesh=fine,
        in_specs=(
            P(DEV, GRP, None),
            P(),
            P(),
            P(),
            P(),
            P(),
            P(),
            P(),
            P(),
            P(),
            P(DEV, None),
            P(None, DEV),
            P(GRP + DEV),
        ),
        out_specs=P(DEV, GRP, None),
        check_vma=False,
    )
```

```python
import functools

import jax
import jax.numpy as jnp
from jax import lax
from jax.experimental import pallas as pl
from jax.experimental.pallas import tpu as pltpu
from jax.sharding import Mesh, PartitionSpec as P

HDIM = 64
GRP = ("zl", "c")
DEV = ("x", "y", "h")
TURNED = ("h", "x", "y")
BF = jnp.bfloat16
F32 = jnp.float32


def rms_scale(row_block, gain_vec):
    widened = row_block.astype(F32)
    inverse = lax.rsqrt(jnp.mean(widened * widened, axis=-1, keepdims=True) + 1e-05)
    return (widened * inverse * gain_vec).astype(BF)


def linear(rows, weight):
    return jnp.dot(rows, weight, preferred_element_type=F32)


def split_heads(rows):
    return rows.reshape(rows.shape[0], -1, HDIM)


def attend(queries, keys, values):
    scores = jnp.einsum("ihd,jhd->hij", queries, keys, preferred_element_type=F32)
    scores = scores * HDIM ** (-0.5)
    exponent = jnp.exp(scores - jnp.max(scores, axis=-1, keepdims=True))
    total = jnp.sum(exponent, axis=-1)
    weighted = jnp.einsum("hij,jhd->ihd", exponent.astype(BF), values, preferred_element_type=F32)
    context = weighted / jnp.transpose(total)[..., None]
    return context.reshape(queries.shape[0], -1).astype(BF)


LOG2E = 1.4426950408889634


def rms_block(rows, gain):
    inverse = lax.rsqrt(jnp.mean(rows * rows, axis=-1, keepdims=True) + 1e-05)
    return (rows * inverse * gain).astype(BF)


def step_of(row, n_flat, n_high, block):
    low, flat = row & (block - 1), (row >> (block.bit_length() - 1)) & (n_flat - 1)
    high = row >> ((block * n_flat).bit_length() - 1)
    return (flat * n_high + high) * block + low


def time_kernel(sizes, start_ref, rows_ref, gain_ref, qk_ref, v_ref, o_ref, out_ref):
    agents, steps, width = rows_ref.shape
    later = step_of(lax.broadcasted_iota(jnp.int32, (steps, 1), 0), *sizes)
    earlier = step_of(lax.broadcasted_iota(jnp.int32, (1, steps), 1), *sizes)
    for agent in range(agents):
        rows = rows_ref[agent].astype(F32)
        normed = rms_block(rows, gain_ref[...])
        queries = linear(normed, qk_ref[0]).astype(BF)
        keys = linear(normed, qk_ref[1]).astype(BF)
        values = linear(normed, v_ref[...]).astype(BF)
        begin = start_ref[agent]
        visible = (later >= earlier) & ((earlier >= begin) | (later < begin))
        context = []
        for h in range(queries.shape[1] // HDIM):
            part = slice(h * HDIM, (h + 1) * HDIM)
            scores = lax.dot_general(
                queries[:, part], keys[:, part], (((1,), (1,)), ((), ())), preferred_element_type=F32
            )
            scores = jnp.where(visible, scores, -jnp.inf)
            top = jnp.max(scores, axis=-1, keepdims=True)
            exponent = jnp.exp2((scores - top) * (LOG2E * HDIM ** (-0.5)))
            total = jnp.sum(exponent, axis=-1, keepdims=True)
            weighted = linear(exponent.astype(BF), values[:, part])
            context.append((weighted / total).astype(BF))
        context = jnp.concatenate(context, 1)
        out_ref[agent] = (rows + linear(context, o_ref[...])).astype(BF)


def time_block(series, sizes, starts, gain, pair, value, out):
    agents, steps, width = series.shape
    vmem = pl.BlockSpec(memory_space=pltpu.VMEM)
    return pl.pallas_call(
        functools.partial(time_kernel, sizes),
        out_shape=jax.ShapeDtypeStruct(series.shape, BF),
        in_specs=[pl.BlockSpec(memory_space=pltpu.SMEM)] + [vmem] * 5,
        out_specs=vmem,
        compiler_params=pltpu.CompilerParams(vmem_limit_bytes=28 << 20),
        cost_estimate=pl.CostEstimate(flops=3 << 30, bytes_accessed=6 << 20, transcendentals=1 << 20),
        name="time_attention",
    )(starts, series, gain[None, :], pair, value, out)


def gelu(x):
    inner = 0.7978845608028654 * (x + 0.044715 * (x * x * x))
    return (0.5 * x) * (1.0 + jnp.tanh(inner))


def ff_kernel(rows_ref, gain_ref, up_ref, down_ref, out_ref, inner, total):
    step, last = pl.program_id(0), pl.num_programs(0) - 1

    @pl.when(step == 0)
    def _():
        rows = rows_ref[...].astype(F32)
        inner[...] = rms_block(rows, gain_ref[...])
        total[...] = rows

    hidden = gelu(linear(inner[...], up_ref[0, 0])).astype(BF)
    total[...] += lax.dot_general(
        hidden, down_ref[0, 0], (((1,), (1,)), ((), ())), preferred_element_type=F32
    )

    @pl.when(step == last)
    def _():
        blocks, agents, block, width = out_ref.shape
        for agent in range(agents):
            part = total[agent * blocks * block : (agent + 1) * blocks * block]
            out_ref[:, agent] = part.reshape(blocks, block, width).astype(BF)


def ff_block(rows, gain, weights, shape):
    rows = rows.reshape(-1, rows.shape[-1])
    count, width = rows.shape
    halves, half = weights.shape[1], weights.shape[3]
    size = 512
    n = half // size
    whole = pl.BlockSpec((count, width), lambda i: (0, 0))
    up = pl.BlockSpec((1, 1, width, size), lambda i: (0, i // n, 0, i % n))
    down = pl.BlockSpec((1, 1, width, size), lambda i: (1, i // n, 0, i % n))
    return pl.pallas_call(
        ff_kernel,
        grid=(halves * n,),
        out_shape=jax.ShapeDtypeStruct(shape, BF),
        in_specs=[whole, pl.BlockSpec((1, width), lambda i: (0, 0)), up, down],
        out_specs=pl.BlockSpec(shape, lambda i: (0, 0, 0, 0)),
        scratch_shapes=[pltpu.VMEM((count, width), BF), pltpu.VMEM((count, width), F32)],
        compiler_params=pltpu.CompilerParams(vmem_limit_bytes=28 << 20),
        cost_estimate=pl.CostEstimate(flops=4 << 30, bytes_accessed=10 << 20, transcendentals=1 << 20),
        name="feed_forward",
    )(rows, gain[None, :], weights, weights)


def pick(places, rows):
    count = rows.shape[0]
    spot = lax.broadcasted_iota(jnp.int32, (places.shape[0], count), 1)
    return linear(jnp.where(spot == places, 1.0, 0.0).astype(BF), rows)


def reorder_kernel(sizes, rows_ref, out_ref):
    n_flat, n_high, own, steps = sizes
    to = lax.broadcasted_iota(jnp.int32, (rows_ref.size // rows_ref.shape[-1], 1), 0)
    bits = lambda n: n.bit_length() - 1
    agent, to = to & (own - 1), to >> bits(own)
    high, to = to & (n_high - 1), to >> bits(n_high)
    flat, step = to & (n_flat - 1), to >> bits(n_flat)
    place = ((high * n_flat + flat) * own + agent) * steps + step
    rows = rows_ref[...].astype(F32).reshape(-1, rows_ref.shape[-1]).astype(BF)
    out_ref[...] = pick(place, rows).reshape(out_ref.shape).astype(BF)


def reorder(sizes, rows, shape):
    vmem = pl.BlockSpec(memory_space=pltpu.VMEM)
    return pl.pallas_call(
        functools.partial(reorder_kernel, sizes),
        out_shape=jax.ShapeDtypeStruct(shape, BF),
        in_specs=[vmem],
        out_specs=vmem,
        compiler_params=pltpu.CompilerParams(vmem_limit_bytes=16 << 20),
        cost_estimate=pl.CostEstimate(flops=1 << 29, bytes_accessed=2 << 20, transcendentals=0),
        name="reorder",
    )(rows)


def other_half(block, zl, high):
    n = lax.axis_size("zl")
    spot = lambda h, z: z * 2 + h
    edge = [(spot(h, z), spot(1 - h, n - 1 - z)) for h in (0, 1) for z in (0, n - 1)]
    inner = [(spot(h, z), spot(h, w)) for h in (0, 1) for z, w in ((0, 1), (n - 1, n - 2))]
    outer = lax.ppermute(block, ("zl", "h"), edge)
    inward = lax.ppermute(outer, ("zl", "h"), inner)
    return jnp.where((zl == 0) | (zl == n - 1), outer, inward)


def on_device(
    rollout,
    agent_gain,
    time_gain,
    inner_gain,
    agent_pair,
    agent_value,
    agent_out,
    time_pair,
    time_value,
    time_out,
    expand_weight,
    reduce_weight,
    episode_start,
):
    steps_here, agents_here, width = rollout.shape
    zl, core, high = lax.axis_index("zl"), lax.axis_index("c"), lax.axis_index("h")
    n_grp, n_core = lax.axis_size(GRP), lax.axis_size("c")

    half = expand_weight.shape[1] // 2
    up = lax.dynamic_slice_in_dim(expand_weight, core * half, half, 1)
    down = lax.dynamic_slice_in_dim(reduce_weight.T, core * half, half, 1)
    mine = jnp.stack([up, down])
    other = other_half(mine, zl, high)

    rows = lax.all_to_all(rollout, GRP, split_axis=0, concat_axis=0, tiled=True)
    rows = rows.reshape(n_grp * agents_here, width)
    pair = jnp.where(
        high == 0, jnp.concatenate([mine, other], 1), jnp.concatenate([other, mine], 1)
    )
    rows, pair = lax.optimization_barrier((rows, pair))
    weights = lax.all_gather(pair, ("c", "x", "y"), axis=1, tiled=True)
    weights = weights.reshape(2, n_core, width, half)

    n_dev = lax.axis_size(DEV)
    agents_own = episode_start.shape[0]
    steps = n_dev * steps_here
    n_high = lax.axis_size("h")
    n_flat = n_dev // n_high
    normed = rms_scale(rows, agent_gain)
    queries = split_heads(linear(normed, agent_pair[0]).astype(BF))
    keys = split_heads(linear(normed, agent_pair[1]).astype(BF))
    values = split_heads(linear(normed, agent_value).astype(BF))
    context = attend(queries, keys, values)
    after_agents = (rows.astype(F32) + linear(context, agent_out)).astype(BF)

    pieces = after_agents.reshape(n_grp, n_flat, n_high, agents_own, width)
    pieces = jnp.transpose(pieces, (2, 1, 0, 3, 4)).reshape(steps, agents_own, width)
    series = lax.all_to_all(pieces, TURNED + GRP, split_axis=0, concat_axis=0, tiled=True)
    series = jnp.swapaxes(series, 0, 1)
    sizes = (n_flat, n_high, steps_here)
    after_time = time_block(
        series, sizes, episode_start, time_gain, time_pair, time_value, time_out
    )
    shape = (n_dev, agents_own, steps_here, width)
    result = ff_block(after_time, inner_gain, weights, shape)
    result = lax.all_to_all(result, TURNED, split_axis=0, concat_axis=0, tiled=True)
    return reorder((n_flat, n_high, agents_own, steps_here), result, rollout.shape)


def solution(mesh):
    fine = Mesh(mesh.devices.reshape(4, 2, 4, 4, 2), ("zl", "c", "x", "y", "h"))
    return jax.shard_map(
        on_device,
        mesh=fine,
        in_specs=(
            P(DEV, GRP, None),
            P(),
            P(),
            P(),
            P(),
            P(),
            P(),
            P(),
            P(),
            P(),
            P(DEV, None),
            P(None, DEV),
            P(GRP + DEV),
        ),
        out_specs=P(DEV, GRP, None),
        check_vma=False,
    )
```

```python
import functools

import jax
import jax.numpy as jnp
from jax import lax
from jax.experimental import pallas as pl
from jax.experimental.pallas import tpu as pltpu
from jax.sharding import Mesh, PartitionSpec as P

HDIM = 64
GRP = ("zl", "c")
DEV = ("x", "y", "h")
TURNED = ("h", "x", "y")
BF = jnp.bfloat16
F32 = jnp.float32


def rms_scale(row_block, gain_vec):
    widened = row_block.astype(F32)
    inverse = lax.rsqrt(jnp.mean(widened * widened, axis=-1, keepdims=True) + 1e-05)
    return (widened * inverse * gain_vec).astype(BF)


def linear(rows, weight):
    return jnp.dot(rows, weight, preferred_element_type=F32)


def split_heads(rows):
    return rows.reshape(rows.shape[0], -1, HDIM)


def attend(queries, keys, values):
    scores = jnp.einsum("ihd,jhd->hij", queries, keys, preferred_element_type=F32)
    scores = scores * HDIM ** (-0.5)
    exponent = jnp.exp(scores - jnp.max(scores, axis=-1, keepdims=True))
    total = jnp.sum(exponent, axis=-1)
    weighted = jnp.einsum("hij,jhd->ihd", exponent.astype(BF), values, preferred_element_type=F32)
    context = weighted / jnp.transpose(total)[..., None]
    return context.reshape(queries.shape[0], -1).astype(BF)


LOG2E = 1.4426950408889634


def rms_block(rows, gain):
    inverse = lax.rsqrt(jnp.mean(rows * rows, axis=-1, keepdims=True) + 1e-05)
    return (rows * inverse * gain).astype(BF)


def step_of(row, n_flat, n_high, block):
    low, flat = row & (block - 1), (row >> (block.bit_length() - 1)) & (n_flat - 1)
    high = row >> ((block * n_flat).bit_length() - 1)
    return (flat * n_high + high) * block + low


def time_kernel(sizes, start_ref, rows_ref, gain_ref, qk_ref, v_ref, o_ref, out_ref):
    agents, steps, width = rows_ref.shape
    later = step_of(lax.broadcasted_iota(jnp.int32, (steps, 1), 0), *sizes)
    earlier = step_of(lax.broadcasted_iota(jnp.int32, (1, steps), 1), *sizes)
    for agent in range(agents):
        rows = rows_ref[agent].astype(F32)
        normed = rms_block(rows, gain_ref[...])
        queries = linear(normed, qk_ref[0]).astype(BF)
        keys = linear(normed, qk_ref[1]).astype(BF)
        values = linear(normed, v_ref[...]).astype(BF)
        begin = start_ref[agent]
        visible = (later >= earlier) & ((earlier >= begin) | (later < begin))
        context = []
        for h in range(queries.shape[1] // HDIM):
            part = slice(h * HDIM, (h + 1) * HDIM)
            scores = lax.dot_general(
                queries[:, part], keys[:, part], (((1,), (1,)), ((), ())), preferred_element_type=F32
            )
            scores = jnp.where(visible, scores, -jnp.inf)
            top = jnp.max(scores, axis=-1, keepdims=True)
            exponent = jnp.exp2((scores - top) * (LOG2E * HDIM ** (-0.5)))
            total = jnp.sum(exponent, axis=-1, keepdims=True)
            weighted = linear(exponent.astype(BF), values[:, part])
            context.append((weighted / total).astype(BF))
        context = jnp.concatenate(context, 1)
        out_ref[agent] = (rows + linear(context, o_ref[...])).astype(BF)


def time_block(series, sizes, starts, gain, pair, value, out):
    agents, steps, width = series.shape
    vmem = pl.BlockSpec(memory_space=pltpu.VMEM)
    return pl.pallas_call(
        functools.partial(time_kernel, sizes),
        out_shape=jax.ShapeDtypeStruct(series.shape, BF),
        in_specs=[pl.BlockSpec(memory_space=pltpu.SMEM)] + [vmem] * 5,
        out_specs=vmem,
        compiler_params=pltpu.CompilerParams(vmem_limit_bytes=28 << 20),
        cost_estimate=pl.CostEstimate(flops=3 << 30, bytes_accessed=6 << 20, transcendentals=1 << 20),
        name="time_attention",
    )(starts, series, gain[None, :], pair, value, out)


def gelu(x):
    inner = 0.7978845608028654 * (x + 0.044715 * (x * x * x))
    return (0.5 * x) * (1.0 + jnp.tanh(inner))


def ff_kernel(rows_ref, gain_ref, up_ref, down_ref, out_ref, inner, total):
    step, last = pl.program_id(0), pl.num_programs(0) - 1

    @pl.when(step == 0)
    def _():
        rows = rows_ref[...].astype(F32)
        inner[...] = rms_block(rows, gain_ref[...])
        total[...] = rows

    hidden = gelu(linear(inner[...], up_ref[0, 0])).astype(BF)
    total[...] += lax.dot_general(
        hidden, down_ref[0, 0], (((1,), (1,)), ((), ())), preferred_element_type=F32
    )

    @pl.when(step == last)
    def _():
        blocks, agents, block, width = out_ref.shape
        for agent in range(agents):
            part = total[agent * blocks * block : (agent + 1) * blocks * block]
            out_ref[:, agent] = part.reshape(blocks, block, width).astype(BF)


def ff_block(rows, gain, weights, shape):
    rows = rows.reshape(-1, rows.shape[-1])
    count, width = rows.shape
    halves, half = weights.shape[1], weights.shape[3]
    size = 512
    n = half // size
    whole = pl.BlockSpec((count, width), lambda i: (0, 0))
    up = pl.BlockSpec((1, 1, width, size), lambda i: (0, i // n, 0, i % n))
    down = pl.BlockSpec((1, 1, width, size), lambda i: (1, i // n, 0, i % n))
    return pl.pallas_call(
        ff_kernel,
        grid=(halves * n,),
        out_shape=jax.ShapeDtypeStruct(shape, BF),
        in_specs=[whole, pl.BlockSpec((1, width), lambda i: (0, 0)), up, down],
        out_specs=pl.BlockSpec(shape, lambda i: (0, 0, 0, 0)),
        scratch_shapes=[pltpu.VMEM((count, width), BF), pltpu.VMEM((count, width), F32)],
        compiler_params=pltpu.CompilerParams(vmem_limit_bytes=28 << 20),
        cost_estimate=pl.CostEstimate(flops=4 << 30, bytes_accessed=10 << 20, transcendentals=1 << 20),
        name="feed_forward",
    )(rows, gain[None, :], weights, weights)


def pick(places, rows):
    count = rows.shape[0]
    spot = lax.broadcasted_iota(jnp.int32, (places.shape[0], count), 1)
    return linear(jnp.where(spot == places, 1.0, 0.0).astype(BF), rows)


def reorder_kernel(sizes, rows_ref, out_ref):
    n_flat, n_high, own, steps = sizes
    to = lax.broadcasted_iota(jnp.int32, (rows_ref.size // rows_ref.shape[-1], 1), 0)
    bits = lambda n: n.bit_length() - 1
    agent, to = to & (own - 1), to >> bits(own)
    high, to = to & (n_high - 1), to >> bits(n_high)
    flat, step = to & (n_flat - 1), to >> bits(n_flat)
    place = ((high * n_flat + flat) * own + agent) * steps + step
    rows = rows_ref[...].astype(F32).reshape(-1, rows_ref.shape[-1]).astype(BF)
    out_ref[...] = pick(place, rows).reshape(out_ref.shape).astype(BF)


def reorder(sizes, rows, shape):
    vmem = pl.BlockSpec(memory_space=pltpu.VMEM)
    return pl.pallas_call(
        functools.partial(reorder_kernel, sizes),
        out_shape=jax.ShapeDtypeStruct(shape, BF),
        in_specs=[vmem],
        out_specs=vmem,
        compiler_params=pltpu.CompilerParams(vmem_limit_bytes=16 << 20),
        cost_estimate=pl.CostEstimate(flops=1 << 29, bytes_accessed=2 << 20, transcendentals=0),
        name="reorder",
    )(rows)


def other_half(block):
    n = lax.axis_size("zl")
    spot = lambda h, z: z * 2 + h
    mirror = [(spot(h, z), spot(1 - h, n - 1 - z)) for h in (0, 1) for z in range(n)]
    return lax.ppermute(block, ("zl", "h"), mirror)


def on_device(
    rollout,
    agent_gain,
    time_gain,
    inner_gain,
    agent_pair,
    agent_value,
    agent_out,
    time_pair,
    time_value,
    time_out,
    expand_weight,
    reduce_weight,
    episode_start,
):
    steps_here, agents_here, width = rollout.shape
    core, high = lax.axis_index("c"), lax.axis_index("h")
    n_grp, n_core = lax.axis_size(GRP), lax.axis_size("c")

    half = expand_weight.shape[1] // 2
    up = lax.dynamic_slice_in_dim(expand_weight, core * half, half, 1)
    down = lax.dynamic_slice_in_dim(reduce_weight.T, core * half, half, 1)
    mine = jnp.stack([up, down])
    other = other_half(mine)

    rows = lax.all_to_all(rollout, GRP, split_axis=0, concat_axis=0, tiled=True)
    rows = rows.reshape(n_grp * agents_here, width)
    pair = jnp.where(
        high == 0, jnp.concatenate([mine, other], 1), jnp.concatenate([other, mine], 1)
    )
    rows, pair = lax.optimization_barrier((rows, pair))
    weights = lax.all_gather(pair, ("c", "x", "y"), axis=1, tiled=True)
    weights = weights.reshape(2, n_core, width, half)

    n_dev = lax.axis_size(DEV)
    agents_own = episode_start.shape[0]
    steps = n_dev * steps_here
    n_high = lax.axis_size("h")
    n_flat = n_dev // n_high
    normed = rms_scale(rows, agent_gain)
    queries = split_heads(linear(normed, agent_pair[0]).astype(BF))
    keys = split_heads(linear(normed, agent_pair[1]).astype(BF))
    values = split_heads(linear(normed, agent_value).astype(BF))
    context = attend(queries, keys, values)
    after_agents = (rows.astype(F32) + linear(context, agent_out)).astype(BF)

    pieces = after_agents.reshape(n_grp, n_flat, n_high, agents_own, width)
    pieces = jnp.transpose(pieces, (2, 1, 0, 3, 4)).reshape(steps, agents_own, width)
    series = lax.all_to_all(pieces, TURNED + GRP, split_axis=0, concat_axis=0, tiled=True)
    series, weights = lax.optimization_barrier((series, weights))
    series = jnp.swapaxes(series, 0, 1)
    sizes = (n_flat, n_high, steps_here)
    after_time = time_block(
        series, sizes, episode_start, time_gain, time_pair, time_value, time_out
    )
    shape = (n_dev, agents_own, steps_here, width)
    result = ff_block(after_time, inner_gain, weights, shape)
    result = lax.all_to_all(result, TURNED, split_axis=0, concat_axis=0, tiled=True)
    return reorder((n_flat, n_high, agents_own, steps_here), result, rollout.shape)


def solution(mesh):
    fine = Mesh(mesh.devices.reshape(4, 2, 4, 4, 2), ("zl", "c", "x", "y", "h"))
    return jax.shard_map(
        on_device,
        mesh=fine,
        in_specs=(
            P(DEV, GRP, None),
            P(),
            P(),
            P(),
            P(),
            P(),
            P(),
            P(),
            P(),
            P(),
            P(DEV, None),
            P(None, DEV),
            P(GRP + DEV),
        ),
        out_specs=P(DEV, GRP, None),
        check_vma=False,
    )
```

```python
import functools

import jax
import jax.numpy as jnp
from jax import lax
from jax.experimental import pallas as pl
from jax.experimental.pallas import tpu as pltpu
from jax.sharding import Mesh, PartitionSpec as P

HDIM = 64
GRP = ("zl", "c")
DEV = ("x", "y", "h")
TURNED = ("h", "x", "y")
BF = jnp.bfloat16
F32 = jnp.float32


def rms_scale(row_block, gain_vec):
    widened = row_block.astype(F32)
    inverse = lax.rsqrt(jnp.mean(widened * widened, axis=-1, keepdims=True) + 1e-05)
    return (widened * inverse * gain_vec).astype(BF)


def linear(rows, weight):
    return jnp.dot(rows, weight, preferred_element_type=F32)


def split_heads(rows):
    return rows.reshape(rows.shape[0], -1, HDIM)


def attend(queries, keys, values):
    scores = jnp.einsum("ihd,jhd->hij", queries, keys, preferred_element_type=F32)
    scores = scores * HDIM ** (-0.5)
    exponent = jnp.exp(scores - jnp.max(scores, axis=-1, keepdims=True))
    total = jnp.sum(exponent, axis=-1)
    weighted = jnp.einsum("hij,jhd->ihd", exponent.astype(BF), values, preferred_element_type=F32)
    context = weighted / jnp.transpose(total)[..., None]
    return context.reshape(queries.shape[0], -1).astype(BF)


LOG2E = 1.4426950408889634


def rms_block(rows, gain):
    inverse = lax.rsqrt(jnp.mean(rows * rows, axis=-1, keepdims=True) + 1e-05)
    return (rows * inverse * gain).astype(BF)


def step_of(row, n_flat, n_high, block):
    low, flat = row & (block - 1), (row >> (block.bit_length() - 1)) & (n_flat - 1)
    high = row >> ((block * n_flat).bit_length() - 1)
    return (flat * n_high + high) * block + low


def time_kernel(sizes, start_ref, rows_ref, gain_ref, qk_ref, v_ref, o_ref, out_ref):
    agents, steps, width = rows_ref.shape
    later = step_of(lax.broadcasted_iota(jnp.int32, (steps, 1), 0), *sizes)
    earlier = step_of(lax.broadcasted_iota(jnp.int32, (1, steps), 1), *sizes)
    for agent in range(agents):
        rows = rows_ref[agent].astype(F32)
        normed = rms_block(rows, gain_ref[...])
        queries = linear(normed, qk_ref[0]).astype(BF)
        keys = linear(normed, qk_ref[1]).astype(BF)
        values = linear(normed, v_ref[...]).astype(BF)
        begin = start_ref[agent]
        visible = (later >= earlier) & ((earlier >= begin) | (later < begin))
        context = []
        for h in range(queries.shape[1] // HDIM):
            part = slice(h * HDIM, (h + 1) * HDIM)
            scores = lax.dot_general(
                queries[:, part], keys[:, part], (((1,), (1,)), ((), ())), preferred_element_type=F32
            )
            scores = jnp.where(visible, scores, -jnp.inf)
            top = jnp.max(scores, axis=-1, keepdims=True)
            exponent = jnp.exp2((scores - top) * (LOG2E * HDIM ** (-0.5)))
            total = jnp.sum(exponent, axis=-1, keepdims=True)
            weighted = linear(exponent.astype(BF), values[:, part])
            context.append((weighted / total).astype(BF))
        context = jnp.concatenate(context, 1)
        out_ref[agent] = (rows + linear(context, o_ref[...])).astype(BF)


def time_block(series, sizes, starts, gain, pair, value, out):
    agents, steps, width = series.shape
    vmem = pl.BlockSpec(memory_space=pltpu.VMEM)
    return pl.pallas_call(
        functools.partial(time_kernel, sizes),
        out_shape=jax.ShapeDtypeStruct(series.shape, BF),
        in_specs=[pl.BlockSpec(memory_space=pltpu.SMEM)] + [vmem] * 5,
        out_specs=vmem,
        compiler_params=pltpu.CompilerParams(vmem_limit_bytes=28 << 20),
        cost_estimate=pl.CostEstimate(flops=3 << 30, bytes_accessed=6 << 20, transcendentals=1 << 20),
        name="time_attention",
    )(starts, series, gain[None, :], pair, value, out)


def gelu(x):
    inner = 0.7978845608028654 * (x + 0.044715 * (x * x * x))
    return (0.5 * x) * (1.0 + jnp.tanh(inner))


def ff_kernel(rows_ref, gain_ref, up_ref, down_ref, out_ref, inner, total):
    step, last = pl.program_id(0), pl.num_programs(0) - 1

    @pl.when(step == 0)
    def _():
        rows = rows_ref[...].astype(F32)
        inner[...] = rms_block(rows, gain_ref[...])
        total[...] = rows

    hidden = gelu(linear(inner[...], up_ref[0, 0])).astype(BF)
    total[...] += lax.dot_general(
        hidden, down_ref[0, 0], (((1,), (1,)), ((), ())), preferred_element_type=F32
    )

    @pl.when(step == last)
    def _():
        blocks, agents, block, width = out_ref.shape
        for agent in range(agents):
            part = total[agent * blocks * block : (agent + 1) * blocks * block]
            out_ref[:, agent] = part.reshape(blocks, block, width).astype(BF)


def ff_block(rows, gain, weights, shape):
    rows = rows.reshape(-1, rows.shape[-1])
    count, width = rows.shape
    halves, half = weights.shape[1], weights.shape[3]
    size = 512
    n = half // size
    whole = pl.BlockSpec((count, width), lambda i: (0, 0))
    up = pl.BlockSpec((1, 1, width, size), lambda i: (0, i // n, 0, i % n))
    down = pl.BlockSpec((1, 1, width, size), lambda i: (1, i // n, 0, i % n))
    return pl.pallas_call(
        ff_kernel,
        grid=(halves * n,),
        out_shape=jax.ShapeDtypeStruct(shape, BF),
        in_specs=[whole, pl.BlockSpec((1, width), lambda i: (0, 0)), up, down],
        out_specs=pl.BlockSpec(shape, lambda i: (0, 0, 0, 0)),
        scratch_shapes=[pltpu.VMEM((count, width), BF), pltpu.VMEM((count, width), F32)],
        compiler_params=pltpu.CompilerParams(vmem_limit_bytes=28 << 20),
        cost_estimate=pl.CostEstimate(flops=4 << 30, bytes_accessed=10 << 20, transcendentals=1 << 20),
        name="feed_forward",
    )(rows, gain[None, :], weights, weights)


def pick(places, rows):
    count = rows.shape[0]
    spot = lax.broadcasted_iota(jnp.int32, (places.shape[0], count), 1)
    return linear(jnp.where(spot == places, 1.0, 0.0).astype(BF), rows)


def reorder_kernel(sizes, rows_ref, out_ref):
    n_flat, n_high, own, steps = sizes
    to = lax.broadcasted_iota(jnp.int32, (rows_ref.size // rows_ref.shape[-1], 1), 0)
    bits = lambda n: n.bit_length() - 1
    agent, to = to & (own - 1), to >> bits(own)
    high, to = to & (n_high - 1), to >> bits(n_high)
    flat, step = to & (n_flat - 1), to >> bits(n_flat)
    place = ((high * n_flat + flat) * own + agent) * steps + step
    rows = rows_ref[...].astype(F32).reshape(-1, rows_ref.shape[-1]).astype(BF)
    out_ref[...] = pick(place, rows).reshape(out_ref.shape).astype(BF)


def reorder(sizes, rows, shape):
    vmem = pl.BlockSpec(memory_space=pltpu.VMEM)
    return pl.pallas_call(
        functools.partial(reorder_kernel, sizes),
        out_shape=jax.ShapeDtypeStruct(shape, BF),
        in_specs=[vmem],
        out_specs=vmem,
        compiler_params=pltpu.CompilerParams(vmem_limit_bytes=16 << 20),
        cost_estimate=pl.CostEstimate(flops=1 << 29, bytes_accessed=2 << 20, transcendentals=0),
        name="reorder",
    )(rows)


def other_half(block):
    n = lax.axis_size("zl")
    spot = lambda h, z: z * 2 + h
    mirror = [(spot(h, z), spot(1 - h, n - 1 - z)) for h in (0, 1) for z in range(n)]
    return lax.ppermute(block, ("zl", "h"), mirror)


def on_device(
    rollout,
    agent_gain,
    time_gain,
    inner_gain,
    agent_pair,
    agent_value,
    agent_out,
    time_pair,
    time_value,
    time_out,
    expand_weight,
    reduce_weight,
    episode_start,
):
    steps_here, agents_here, width = rollout.shape
    core, high = lax.axis_index("c"), lax.axis_index("h")
    n_grp, n_core = lax.axis_size(GRP), lax.axis_size("c")

    half = expand_weight.shape[1] // 2
    up = lax.dynamic_slice_in_dim(expand_weight, core * half, half, 1)
    down = lax.dynamic_slice_in_dim(reduce_weight.T, core * half, half, 1)
    mine = jnp.stack([up, down])
    other = other_half(mine)

    odd = mine[0, 0, 0] != mine[0, 0, 0]
    rows = jnp.where(odd, -rollout, rollout)
    rows = lax.all_to_all(rows, GRP, split_axis=0, concat_axis=0, tiled=True)
    rows = rows.reshape(n_grp * agents_here, width)
    pair = jnp.where(
        high == 0, jnp.concatenate([mine, other], 1), jnp.concatenate([other, mine], 1)
    )
    weights = lax.all_gather(pair, ("c", "x", "y"), axis=1, tiled=True)
    weights = weights.reshape(2, n_core, width, half)

    n_dev = lax.axis_size(DEV)
    agents_own = episode_start.shape[0]
    steps = n_dev * steps_here
    n_high = lax.axis_size("h")
    n_flat = n_dev // n_high
    normed = rms_scale(rows, agent_gain)
    queries = split_heads(linear(normed, agent_pair[0]).astype(BF))
    keys = split_heads(linear(normed, agent_pair[1]).astype(BF))
    values = split_heads(linear(normed, agent_value).astype(BF))
    context = attend(queries, keys, values)
    after_agents = (rows.astype(F32) + linear(context, agent_out)).astype(BF)

    pieces = after_agents.reshape(n_grp, n_flat, n_high, agents_own, width)
    pieces = jnp.transpose(pieces, (2, 1, 0, 3, 4)).reshape(steps, agents_own, width)
    series = lax.all_to_all(pieces, TURNED + GRP, split_axis=0, concat_axis=0, tiled=True)
    series, weights = lax.optimization_barrier((series, weights))
    series = jnp.swapaxes(series, 0, 1)
    sizes = (n_flat, n_high, steps_here)
    after_time = time_block(
        series, sizes, episode_start, time_gain, time_pair, time_value, time_out
    )
    shape = (n_dev, agents_own, steps_here, width)
    result = ff_block(after_time, inner_gain, weights, shape)
    result = lax.all_to_all(result, TURNED, split_axis=0, concat_axis=0, tiled=True)
    return reorder((n_flat, n_high, agents_own, steps_here), result, rollout.shape)


def solution(mesh):
    fine = Mesh(mesh.devices.reshape(4, 2, 4, 4, 2), ("zl", "c", "x", "y", "h"))
    return jax.shard_map(
        on_device,
        mesh=fine,
        in_specs=(
            P(DEV, GRP, None),
            P(),
            P(),
            P(),
            P(),
            P(),
            P(),
            P(),
            P(),
            P(),
            P(DEV, None),
            P(None, DEV),
            P(GRP + DEV),
        ),
        out_specs=P(DEV, GRP, None),
        check_vma=False,
    )
```

```python
import functools

import jax
import jax.numpy as jnp
from jax import lax
from jax.experimental import pallas as pl
from jax.experimental.pallas import tpu as pltpu
from jax.sharding import Mesh, PartitionSpec as P

HDIM = 64
GRP = ("zl", "c")
DEV = ("x", "y", "h")
TURNED = ("h", "x", "y")
BF = jnp.bfloat16
F32 = jnp.float32


def rms_scale(row_block, gain_vec):
    widened = row_block.astype(F32)
    inverse = lax.rsqrt(jnp.mean(widened * widened, axis=-1, keepdims=True) + 1e-05)
    return (widened * inverse * gain_vec).astype(BF)


def linear(rows, weight):
    return jnp.dot(rows, weight, preferred_element_type=F32)


def split_heads(rows):
    return rows.reshape(rows.shape[0], -1, HDIM)


def attend(queries, keys, values):
    scores = jnp.einsum("ihd,jhd->hij", queries, keys, preferred_element_type=F32)
    scores = scores * HDIM ** (-0.5)
    exponent = jnp.exp(scores - jnp.max(scores, axis=-1, keepdims=True))
    total = jnp.sum(exponent, axis=-1)
    weighted = jnp.einsum("hij,jhd->ihd", exponent.astype(BF), values, preferred_element_type=F32)
    context = weighted / jnp.transpose(total)[..., None]
    return context.reshape(queries.shape[0], -1).astype(BF)


LOG2E = 1.4426950408889634


def rms_block(rows, gain):
    inverse = lax.rsqrt(jnp.mean(rows * rows, axis=-1, keepdims=True) + 1e-05)
    return (rows * inverse * gain).astype(BF)


def step_of(row, n_flat, n_high, block):
    low, flat = row & (block - 1), (row >> (block.bit_length() - 1)) & (n_flat - 1)
    high = row >> ((block * n_flat).bit_length() - 1)
    return (flat * n_high + high) * block + low


def time_kernel(sizes, start_ref, rows_ref, gain_ref, qk_ref, v_ref, o_ref, out_ref):
    agents, steps, width = rows_ref.shape
    later = step_of(lax.broadcasted_iota(jnp.int32, (steps, 1), 0), *sizes)
    earlier = step_of(lax.broadcasted_iota(jnp.int32, (1, steps), 1), *sizes)
    rows = jnp.concatenate([rows_ref[agent].astype(F32) for agent in range(agents)], 0)
    normed = rms_block(rows, gain_ref[...])
    queries = linear(normed, qk_ref[0]).astype(BF)
    keys = linear(normed, qk_ref[1]).astype(BF)
    values = linear(normed, v_ref[...]).astype(BF)
    context = []
    for agent in range(agents):
        begin = start_ref[agent]
        visible = (later >= earlier) & ((earlier >= begin) | (later < begin))
        own = slice(agent * steps, (agent + 1) * steps)
        parts = []
        for h in range(queries.shape[1] // HDIM):
            part = slice(h * HDIM, (h + 1) * HDIM)
            scores = lax.dot_general(
                queries[own, part], keys[own, part], (((1,), (1,)), ((), ())), preferred_element_type=F32
            )
            scores = jnp.where(visible, scores, -jnp.inf)
            top = jnp.max(scores, axis=-1, keepdims=True)
            exponent = jnp.exp2((scores - top) * (LOG2E * HDIM ** (-0.5)))
            total = jnp.sum(exponent, axis=-1, keepdims=True)
            weighted = linear(exponent.astype(BF), values[own, part])
            parts.append((weighted / total).astype(BF))
        context.append(jnp.concatenate(parts, 1))
    result = (rows + linear(jnp.concatenate(context, 0), o_ref[...])).astype(BF)
    for agent in range(agents):
        out_ref[agent] = result[agent * steps : (agent + 1) * steps]


def time_block(series, sizes, starts, gain, pair, value, out):
    agents, steps, width = series.shape
    vmem = pl.BlockSpec(memory_space=pltpu.VMEM)
    return pl.pallas_call(
        functools.partial(time_kernel, sizes),
        out_shape=jax.ShapeDtypeStruct(series.shape, BF),
        in_specs=[pl.BlockSpec(memory_space=pltpu.SMEM)] + [vmem] * 5,
        out_specs=vmem,
        compiler_params=pltpu.CompilerParams(vmem_limit_bytes=28 << 20),
        cost_estimate=pl.CostEstimate(flops=3 << 30, bytes_accessed=6 << 20, transcendentals=1 << 20),
        name="time_attention",
    )(starts, series, gain[None, :], pair, value, out)


def gelu(x):
    inner = 0.7978845608028654 * (x + 0.044715 * (x * x * x))
    return (0.5 * x) * (1.0 + jnp.tanh(inner))


def ff_kernel(rows_ref, gain_ref, up_ref, down_ref, out_ref, inner, total):
    step, last = pl.program_id(0), pl.num_programs(0) - 1

    @pl.when(step == 0)
    def _():
        rows = rows_ref[...].astype(F32)
        inner[...] = rms_block(rows, gain_ref[...])
        total[...] = rows

    hidden = gelu(linear(inner[...], up_ref[0, 0])).astype(BF)
    total[...] += lax.dot_general(
        hidden, down_ref[0, 0], (((1,), (1,)), ((), ())), preferred_element_type=F32
    )

    @pl.when(step == last)
    def _():
        blocks, agents, block, width = out_ref.shape
        for agent in range(agents):
            part = total[agent * blocks * block : (agent + 1) * blocks * block]
            out_ref[:, agent] = part.reshape(blocks, block, width).astype(BF)


def ff_block(rows, gain, weights, shape):
    rows = rows.reshape(-1, rows.shape[-1])
    count, width = rows.shape
    halves, half = weights.shape[1], weights.shape[3]
    size = 512
    n = half // size
    whole = pl.BlockSpec((count, width), lambda i: (0, 0))
    up = pl.BlockSpec((1, 1, width, size), lambda i: (0, i // n, 0, i % n))
    down = pl.BlockSpec((1, 1, width, size), lambda i: (1, i // n, 0, i % n))
    return pl.pallas_call(
        ff_kernel,
        grid=(halves * n,),
        out_shape=jax.ShapeDtypeStruct(shape, BF),
        in_specs=[whole, pl.BlockSpec((1, width), lambda i: (0, 0)), up, down],
        out_specs=pl.BlockSpec(shape, lambda i: (0, 0, 0, 0)),
        scratch_shapes=[pltpu.VMEM((count, width), BF), pltpu.VMEM((count, width), F32)],
        compiler_params=pltpu.CompilerParams(vmem_limit_bytes=28 << 20),
        cost_estimate=pl.CostEstimate(flops=4 << 30, bytes_accessed=10 << 20, transcendentals=1 << 20),
        name="feed_forward",
    )(rows, gain[None, :], weights, weights)


def pick(places, rows):
    count = rows.shape[0]
    spot = lax.broadcasted_iota(jnp.int32, (places.shape[0], count), 1)
    return linear(jnp.where(spot == places, 1.0, 0.0).astype(BF), rows)


def reorder_kernel(sizes, rows_ref, out_ref):
    n_flat, n_high, own, steps = sizes
    to = lax.broadcasted_iota(jnp.int32, (rows_ref.size // rows_ref.shape[-1], 1), 0)
    bits = lambda n: n.bit_length() - 1
    agent, to = to & (own - 1), to >> bits(own)
    high, to = to & (n_high - 1), to >> bits(n_high)
    flat, step = to & (n_flat - 1), to >> bits(n_flat)
    place = ((high * n_flat + flat) * own + agent) * steps + step
    rows = rows_ref[...].astype(F32).reshape(-1, rows_ref.shape[-1]).astype(BF)
    out_ref[...] = pick(place, rows).reshape(out_ref.shape).astype(BF)


def reorder(sizes, rows, shape):
    vmem = pl.BlockSpec(memory_space=pltpu.VMEM)
    return pl.pallas_call(
        functools.partial(reorder_kernel, sizes),
        out_shape=jax.ShapeDtypeStruct(shape, BF),
        in_specs=[vmem],
        out_specs=vmem,
        compiler_params=pltpu.CompilerParams(vmem_limit_bytes=16 << 20),
        cost_estimate=pl.CostEstimate(flops=1 << 29, bytes_accessed=2 << 20, transcendentals=0),
        name="reorder",
    )(rows)


def other_half(block):
    n = lax.axis_size("zl")
    spot = lambda h, z: z * 2 + h
    mirror = [(spot(h, z), spot(1 - h, n - 1 - z)) for h in (0, 1) for z in range(n)]
    return lax.ppermute(block, ("zl", "h"), mirror)


def on_device(
    rollout,
    agent_gain,
    time_gain,
    inner_gain,
    agent_pair,
    agent_value,
    agent_out,
    time_pair,
    time_value,
    time_out,
    expand_weight,
    reduce_weight,
    episode_start,
):
    steps_here, agents_here, width = rollout.shape
    core, high = lax.axis_index("c"), lax.axis_index("h")
    n_grp, n_core = lax.axis_size(GRP), lax.axis_size("c")

    half = expand_weight.shape[1] // 2
    up = lax.dynamic_slice_in_dim(expand_weight, core * half, half, 1)
    down = lax.dynamic_slice_in_dim(reduce_weight.T, core * half, half, 1)
    mine = jnp.stack([up, down])
    other = other_half(mine)

    rows = lax.all_to_all(rollout, GRP, split_axis=0, concat_axis=0, tiled=True)
    rows = rows.reshape(n_grp * agents_here, width)
    pair = jnp.where(
        high == 0, jnp.concatenate([mine, other], 1), jnp.concatenate([other, mine], 1)
    )
    weights = lax.all_gather(pair, ("c", "x", "y"), axis=1, tiled=True)
    weights = weights.reshape(2, n_core, width, half)
    rows, other = lax.optimization_barrier((rows, other))

    n_dev = lax.axis_size(DEV)
    agents_own = episode_start.shape[0]
    steps = n_dev * steps_here
    n_high = lax.axis_size("h")
    n_flat = n_dev // n_high
    normed = rms_scale(rows, agent_gain)
    queries = split_heads(linear(normed, agent_pair[0]).astype(BF))
    keys = split_heads(linear(normed, agent_pair[1]).astype(BF))
    values = split_heads(linear(normed, agent_value).astype(BF))
    context = attend(queries, keys, values)
    after_agents = (rows.astype(F32) + linear(context, agent_out)).astype(BF)

    pieces = after_agents.reshape(n_grp, n_flat, n_high, agents_own, width)
    pieces = jnp.transpose(pieces, (2, 1, 0, 3, 4)).reshape(steps, agents_own, width)
    series = lax.all_to_all(pieces, TURNED + GRP, split_axis=0, concat_axis=0, tiled=True)
    series = jnp.swapaxes(series, 0, 1)
    sizes = (n_flat, n_high, steps_here)
    after_time = time_block(
        series, sizes, episode_start, time_gain, time_pair, time_value, time_out
    )
    shape = (n_dev, agents_own, steps_here, width)
    result = ff_block(after_time, inner_gain, weights, shape)
    result = lax.all_to_all(result, TURNED, split_axis=0, concat_axis=0, tiled=True)
    return reorder((n_flat, n_high, agents_own, steps_here), result, rollout.shape)


def solution(mesh):
    fine = Mesh(mesh.devices.reshape(4, 2, 4, 4, 2), ("zl", "c", "x", "y", "h"))
    return jax.shard_map(
        on_device,
        mesh=fine,
        in_specs=(
            P(DEV, GRP, None),
            P(),
            P(),
            P(),
            P(),
            P(),
            P(),
            P(),
            P(),
            P(),
            P(DEV, None),
            P(None, DEV),
            P(GRP + DEV),
        ),
        out_specs=P(DEV, GRP, None),
        check_vma=False,
    )
```

```python
import functools

import jax
import jax.numpy as jnp
from jax import lax
from jax.experimental import pallas as pl
from jax.experimental.pallas import tpu as pltpu
from jax.sharding import Mesh, PartitionSpec as P

HDIM = 64
GRP = ("zl", "c")
DEV = ("x", "y", "h")
TURNED = ("h", "x", "y")
BF = jnp.bfloat16
F32 = jnp.float32


def rms_scale(row_block, gain_vec):
    widened = row_block.astype(F32)
    inverse = lax.rsqrt(jnp.mean(widened * widened, axis=-1, keepdims=True) + 1e-05)
    return (widened * inverse * gain_vec).astype(BF)


def linear(rows, weight):
    return jnp.dot(rows, weight, preferred_element_type=F32)


def split_heads(rows):
    return rows.reshape(rows.shape[0], -1, HDIM)


def attend(queries, keys, values):
    scores = jnp.einsum("ihd,jhd->hij", queries, keys, preferred_element_type=F32)
    scores = scores * HDIM ** (-0.5)
    exponent = jnp.exp(scores - jnp.max(scores, axis=-1, keepdims=True))
    total = jnp.sum(exponent, axis=-1)
    weighted = jnp.einsum("hij,jhd->ihd", exponent.astype(BF), values, preferred_element_type=F32)
    context = weighted / jnp.transpose(total)[..., None]
    return context.reshape(queries.shape[0], -1).astype(BF)


LOG2E = 1.4426950408889634


def rms_block(rows, gain):
    inverse = lax.rsqrt(jnp.mean(rows * rows, axis=-1, keepdims=True) + 1e-05)
    return (rows * inverse * gain).astype(BF)


def step_of(row, n_flat, n_high, block):
    low, flat = row & (block - 1), (row >> (block.bit_length() - 1)) & (n_flat - 1)
    high = row >> ((block * n_flat).bit_length() - 1)
    return (flat * n_high + high) * block + low


def time_kernel(sizes, start_ref, rows_ref, gain_ref, qk_ref, v_ref, o_ref, out_ref):
    agents, steps, width = rows_ref.shape
    later = step_of(lax.broadcasted_iota(jnp.int32, (steps, 1), 0), *sizes)
    earlier = step_of(lax.broadcasted_iota(jnp.int32, (1, steps), 1), *sizes)
    rows = jnp.concatenate([rows_ref[agent].astype(F32) for agent in range(agents)], 0)
    normed = rms_block(rows, gain_ref[...])
    queries = linear(normed, qk_ref[0]).astype(BF)
    keys = linear(normed, qk_ref[1]).astype(BF)
    values = linear(normed, v_ref[...]).astype(BF)
    context = []
    for agent in range(agents):
        begin = start_ref[agent]
        visible = (later >= earlier) & ((earlier >= begin) | (later < begin))
        own = slice(agent * steps, (agent + 1) * steps)
        parts = []
        for h in range(queries.shape[1] // HDIM):
            part = slice(h * HDIM, (h + 1) * HDIM)
            scores = lax.dot_general(
                queries[own, part], keys[own, part], (((1,), (1,)), ((), ())), preferred_element_type=F32
            )
            scores = jnp.where(visible, scores, -jnp.inf)
            top = jnp.max(scores, axis=-1, keepdims=True)
            exponent = jnp.exp2((scores - top) * (LOG2E * HDIM ** (-0.5)))
            total = jnp.sum(exponent, axis=-1, keepdims=True)
            weighted = linear(exponent.astype(BF), values[own, part])
            parts.append((weighted / total).astype(BF))
        context.append(jnp.concatenate(parts, 1))
    result = (rows + linear(jnp.concatenate(context, 0), o_ref[...])).astype(BF)
    for agent in range(agents):
        out_ref[agent] = result[agent * steps : (agent + 1) * steps]


def time_block(series, sizes, starts, gain, pair, value, out):
    agents, steps, width = series.shape
    vmem = pl.BlockSpec(memory_space=pltpu.VMEM)
    return pl.pallas_call(
        functools.partial(time_kernel, sizes),
        out_shape=jax.ShapeDtypeStruct(series.shape, BF),
        in_specs=[pl.BlockSpec(memory_space=pltpu.SMEM)] + [vmem] * 5,
        out_specs=vmem,
        compiler_params=pltpu.CompilerParams(vmem_limit_bytes=28 << 20),
        cost_estimate=pl.CostEstimate(flops=3 << 30, bytes_accessed=6 << 20, transcendentals=1 << 20),
        name="time_attention",
    )(starts, series, gain[None, :], pair, value, out)


def gelu(x):
    inner = 0.7978845608028654 * (x + 0.044715 * (x * x * x))
    return (0.5 * x) * (1.0 + jnp.tanh(inner))


def ff_kernel(rows_ref, gain_ref, weights_ref, out_ref, held, arrived):
    halves, width, half = weights_ref.shape[1:]
    size = half // 2
    parts = [(i, j) for i in range(halves) for j in range(half // size)]

    def fetch(n, which):
        i, j = parts[n]
        source = weights_ref.at[which, i, :, pl.ds(j * size, size)]
        return pltpu.make_async_copy(source, held.at[n, which], arrived.at[n, which])

    fetch(0, 0).start()
    fetch(0, 1).start()
    total = rows_ref[...].astype(F32)
    inner = rms_block(total, gain_ref[...])
    for n in range(len(parts)):
        fetch(n, 0).wait()
        if n + 1 < len(parts):
            fetch(n + 1, 0).start()
            fetch(n + 1, 1).start()
        hidden = gelu(linear(inner, held[n, 0])).astype(BF)
        fetch(n, 1).wait()
        total = total + lax.dot_general(
            hidden, held[n, 1], (((1,), (1,)), ((), ())), preferred_element_type=F32
        )
    blocks, agents, block, _ = out_ref.shape
    for agent in range(agents):
        part = total[agent * blocks * block : (agent + 1) * blocks * block]
        out_ref[:, agent] = part.reshape(blocks, block, width).astype(BF)


def ff_block(rows, gain, weights, shape):
    rows = rows.reshape(-1, rows.shape[-1])
    halves, width, half = weights.shape[1:]
    vmem = pl.BlockSpec(memory_space=pltpu.VMEM)
    return pl.pallas_call(
        ff_kernel,
        out_shape=jax.ShapeDtypeStruct(shape, BF),
        in_specs=[vmem, vmem, pl.BlockSpec(memory_space=pltpu.HBM)],
        out_specs=vmem,
        scratch_shapes=[
            pltpu.VMEM((2 * halves, 2, width, half // 2), BF),
            pltpu.SemaphoreType.DMA((2 * halves, 2)),
        ],
        compiler_params=pltpu.CompilerParams(vmem_limit_bytes=50 << 20),
        cost_estimate=pl.CostEstimate(flops=4 << 30, bytes_accessed=10 << 20, transcendentals=1 << 20),
        name="feed_forward",
    )(rows, gain[None, :], weights)


def pick(places, rows):
    count = rows.shape[0]
    spot = lax.broadcasted_iota(jnp.int32, (places.shape[0], count), 1)
    return linear(jnp.where(spot == places, 1.0, 0.0).astype(BF), rows)


def reorder_kernel(sizes, rows_ref, out_ref):
    n_flat, n_high, own, steps = sizes
    to = lax.broadcasted_iota(jnp.int32, (rows_ref.size // rows_ref.shape[-1], 1), 0)
    bits = lambda n: n.bit_length() - 1
    agent, to = to & (own - 1), to >> bits(own)
    high, to = to & (n_high - 1), to >> bits(n_high)
    flat, step = to & (n_flat - 1), to >> bits(n_flat)
    place = ((high * n_flat + flat) * own + agent) * steps + step
    rows = rows_ref[...].astype(F32).reshape(-1, rows_ref.shape[-1]).astype(BF)
    out_ref[...] = pick(place, rows).reshape(out_ref.shape).astype(BF)


def reorder(sizes, rows, shape):
    vmem = pl.BlockSpec(memory_space=pltpu.VMEM)
    return pl.pallas_call(
        functools.partial(reorder_kernel, sizes),
        out_shape=jax.ShapeDtypeStruct(shape, BF),
        in_specs=[vmem],
        out_specs=vmem,
        compiler_params=pltpu.CompilerParams(vmem_limit_bytes=16 << 20),
        cost_estimate=pl.CostEstimate(flops=1 << 29, bytes_accessed=2 << 20, transcendentals=0),
        name="reorder",
    )(rows)


def other_half(block):
    n = lax.axis_size("zl")
    spot = lambda h, z: z * 2 + h
    mirror = [(spot(h, z), spot(1 - h, n - 1 - z)) for h in (0, 1) for z in range(n)]
    return lax.ppermute(block, ("zl", "h"), mirror)


def on_device(
    rollout,
    agent_gain,
    time_gain,
    inner_gain,
    agent_pair,
    agent_value,
    agent_out,
    time_pair,
    time_value,
    time_out,
    expand_weight,
    reduce_weight,
    episode_start,
):
    steps_here, agents_here, width = rollout.shape
    core, high = lax.axis_index("c"), lax.axis_index("h")
    n_grp, n_core = lax.axis_size(GRP), lax.axis_size("c")

    half = expand_weight.shape[1] // 2
    up = lax.dynamic_slice_in_dim(expand_weight, core * half, half, 1)
    down = lax.dynamic_slice_in_dim(reduce_weight.T, core * half, half, 1)
    mine = jnp.stack([up, down])
    other = other_half(mine)

    rows = lax.all_to_all(rollout, GRP, split_axis=0, concat_axis=0, tiled=True)
    rows = rows.reshape(n_grp * agents_here, width)
    pair = jnp.where(
        high == 0, jnp.concatenate([mine, other], 1), jnp.concatenate([other, mine], 1)
    )
    rows, pair = lax.optimization_barrier((rows, pair))
    weights = lax.all_gather(pair, ("c", "x", "y"), axis=1, tiled=True)
    weights = weights.reshape(2, n_core, width, half)

    n_dev = lax.axis_size(DEV)
    agents_own = episode_start.shape[0]
    steps = n_dev * steps_here
    n_high = lax.axis_size("h")
    n_flat = n_dev // n_high
    normed = rms_scale(rows, agent_gain)
    queries = split_heads(linear(normed, agent_pair[0]).astype(BF))
    keys = split_heads(linear(normed, agent_pair[1]).astype(BF))
    values = split_heads(linear(normed, agent_value).astype(BF))
    context = attend(queries, keys, values)
    after_agents = (rows.astype(F32) + linear(context, agent_out)).astype(BF)

    pieces = after_agents.reshape(n_grp, n_flat, n_high, agents_own, width)
    pieces = jnp.transpose(pieces, (2, 1, 0, 3, 4)).reshape(steps, agents_own, width)
    series = lax.all_to_all(pieces, TURNED + GRP, split_axis=0, concat_axis=0, tiled=True)
    series = jnp.swapaxes(series, 0, 1)
    sizes = (n_flat, n_high, steps_here)
    after_time = time_block(
        series, sizes, episode_start, time_gain, time_pair, time_value, time_out
    )
    shape = (n_dev, agents_own, steps_here, width)
    result = ff_block(after_time, inner_gain, weights, shape)
    result = lax.all_to_all(result, TURNED, split_axis=0, concat_axis=0, tiled=True)
    return reorder((n_flat, n_high, agents_own, steps_here), result, rollout.shape)


def solution(mesh):
    fine = Mesh(mesh.devices.reshape(4, 2, 4, 4, 2), ("zl", "c", "x", "y", "h"))
    return jax.shard_map(
        on_device,
        mesh=fine,
        in_specs=(
            P(DEV, GRP, None),
            P(),
            P(),
            P(),
            P(),
            P(),
            P(),
            P(),
            P(),
            P(),
            P(DEV, None),
            P(None, DEV),
            P(GRP + DEV),
        ),
        out_specs=P(DEV, GRP, None),
        check_vma=False,
    )
```

```python
import functools

import jax
import jax.numpy as jnp
from jax import lax
from jax.experimental import pallas as pl
from jax.experimental.pallas import tpu as pltpu
from jax.sharding import Mesh, PartitionSpec as P

HDIM = 64
GRP = ("zl", "c")
DEV = ("x", "y", "h")
TURNED = ("h", "x", "y")
BF = jnp.bfloat16
F32 = jnp.float32


def rms_scale(row_block, gain_vec):
    widened = row_block.astype(F32)
    inverse = lax.rsqrt(jnp.mean(widened * widened, axis=-1, keepdims=True) + 1e-05)
    return (widened * inverse * gain_vec).astype(BF)


def linear(rows, weight):
    return jnp.dot(rows, weight, preferred_element_type=F32)


def split_heads(rows):
    return rows.reshape(rows.shape[0], -1, HDIM)


def attend(queries, keys, values):
    scores = jnp.einsum("ihd,jhd->hij", queries, keys, preferred_element_type=F32)
    scores = scores * HDIM ** (-0.5)
    exponent = jnp.exp(scores - jnp.max(scores, axis=-1, keepdims=True))
    total = jnp.sum(exponent, axis=-1)
    weighted = jnp.einsum("hij,jhd->ihd", exponent.astype(BF), values, preferred_element_type=F32)
    context = weighted / jnp.transpose(total)[..., None]
    return context.reshape(queries.shape[0], -1).astype(BF)


LOG2E = 1.4426950408889634


def rms_block(rows, gain):
    inverse = lax.rsqrt(jnp.mean(rows * rows, axis=-1, keepdims=True) + 1e-05)
    return (rows * inverse * gain).astype(BF)


def step_of(row, n_flat, n_high, block):
    low, flat = row & (block - 1), (row >> (block.bit_length() - 1)) & (n_flat - 1)
    high = row >> ((block * n_flat).bit_length() - 1)
    return (flat * n_high + high) * block + low


def time_kernel(sizes, start_ref, rows_ref, gain_ref, qk_ref, v_ref, o_ref, out_ref):
    agents, steps, width = rows_ref.shape
    later = step_of(lax.broadcasted_iota(jnp.int32, (steps, 1), 0), *sizes)
    earlier = step_of(lax.broadcasted_iota(jnp.int32, (1, steps), 1), *sizes)
    rows = jnp.concatenate([rows_ref[agent].astype(F32) for agent in range(agents)], 0)
    normed = rms_block(rows, gain_ref[...])
    queries = linear(normed, qk_ref[0]).astype(BF)
    keys = linear(normed, qk_ref[1]).astype(BF)
    values = linear(normed, v_ref[...]).astype(BF)
    context = []
    for agent in range(agents):
        begin = start_ref[agent]
        visible = (later >= earlier) & ((earlier >= begin) | (later < begin))
        own = slice(agent * steps, (agent + 1) * steps)
        parts = []
        for h in range(queries.shape[1] // HDIM):
            part = slice(h * HDIM, (h + 1) * HDIM)
            scores = lax.dot_general(
                queries[own, part], keys[own, part], (((1,), (1,)), ((), ())), preferred_element_type=F32
            )
            scores = jnp.where(visible, scores, -jnp.inf)
            top = jnp.max(scores, axis=-1, keepdims=True)
            exponent = jnp.exp2((scores - top) * (LOG2E * HDIM ** (-0.5)))
            total = jnp.sum(exponent, axis=-1, keepdims=True)
            weighted = linear(exponent.astype(BF), values[own, part])
            parts.append((weighted / total).astype(BF))
        context.append(jnp.concatenate(parts, 1))
    result = (rows + linear(jnp.concatenate(context, 0), o_ref[...])).astype(BF)
    for agent in range(agents):
        out_ref[agent] = result[agent * steps : (agent + 1) * steps]


def time_block(series, sizes, starts, gain, pair, value, out):
    agents, steps, width = series.shape
    vmem = pl.BlockSpec(memory_space=pltpu.VMEM)
    return pl.pallas_call(
        functools.partial(time_kernel, sizes),
        out_shape=jax.ShapeDtypeStruct(series.shape, BF),
        in_specs=[pl.BlockSpec(memory_space=pltpu.SMEM)] + [vmem] * 5,
        out_specs=vmem,
        compiler_params=pltpu.CompilerParams(vmem_limit_bytes=28 << 20),
        cost_estimate=pl.CostEstimate(flops=3 << 30, bytes_accessed=6 << 20, transcendentals=1 << 20),
        name="time_attention",
    )(starts, series, gain[None, :], pair, value, out)


def gelu(x):
    inner = 0.7978845608028654 * (x + 0.044715 * (x * x * x))
    return (0.5 * x) * (1.0 + jnp.tanh(inner))


def ff_kernel(rows_ref, gain_ref, weights_ref, out_ref, held, arrived):
    halves, shards, _, depth, half = weights_ref.shape
    width, size = shards * depth, half // 2
    parts = [(i, j) for i in range(halves) for j in range(half // size)]

    def fetch(n, which):
        i, j = parts[n]
        source = weights_ref.at[i, :, which, :, pl.ds(j * size, size)]
        return pltpu.make_async_copy(source, held.at[n, which], arrived.at[n, which])

    fetch(0, 0).start()
    fetch(0, 1).start()
    total = rows_ref[...].astype(F32)
    inner = rms_block(total, gain_ref[...])
    for n in range(len(parts)):
        fetch(n, 0).wait()
        if n + 1 < len(parts):
            fetch(n + 1, 0).start()
            fetch(n + 1, 1).start()
        hidden = gelu(linear(inner, held[n, 0].reshape(width, size))).astype(BF)
        fetch(n, 1).wait()
        total = total + lax.dot_general(
            hidden,
            held[n, 1].reshape(width, size),
            (((1,), (1,)), ((), ())),
            preferred_element_type=F32,
        )
    blocks, agents, block, _ = out_ref.shape
    for agent in range(agents):
        part = total[agent * blocks * block : (agent + 1) * blocks * block]
        out_ref[:, agent] = part.reshape(blocks, block, width).astype(BF)


def ff_block(rows, gain, weights, shape):
    rows = rows.reshape(-1, rows.shape[-1])
    halves, shards, _, depth, half = weights.shape
    vmem = pl.BlockSpec(memory_space=pltpu.VMEM)
    return pl.pallas_call(
        ff_kernel,
        out_shape=jax.ShapeDtypeStruct(shape, BF),
        in_specs=[vmem, vmem, pl.BlockSpec(memory_space=pltpu.HBM)],
        out_specs=vmem,
        scratch_shapes=[
            pltpu.VMEM((2 * halves, 2, shards, depth, half // 2), BF),
            pltpu.SemaphoreType.DMA((2 * halves, 2)),
        ],
        compiler_params=pltpu.CompilerParams(vmem_limit_bytes=50 << 20),
        cost_estimate=pl.CostEstimate(flops=4 << 30, bytes_accessed=10 << 20, transcendentals=1 << 20),
        name="feed_forward",
    )(rows, gain[None, :], weights)


def pick(places, rows):
    count = rows.shape[0]
    spot = lax.broadcasted_iota(jnp.int32, (places.shape[0], count), 1)
    return linear(jnp.where(spot == places, 1.0, 0.0).astype(BF), rows)


def reorder_kernel(sizes, rows_ref, out_ref):
    n_flat, n_high, own, steps = sizes
    to = lax.broadcasted_iota(jnp.int32, (rows_ref.size // rows_ref.shape[-1], 1), 0)
    bits = lambda n: n.bit_length() - 1
    agent, to = to & (own - 1), to >> bits(own)
    high, to = to & (n_high - 1), to >> bits(n_high)
    flat, step = to & (n_flat - 1), to >> bits(n_flat)
    place = ((high * n_flat + flat) * own + agent) * steps + step
    rows = rows_ref[...].astype(F32).reshape(-1, rows_ref.shape[-1]).astype(BF)
    out_ref[...] = pick(place, rows).reshape(out_ref.shape).astype(BF)


def reorder(sizes, rows, shape):
    vmem = pl.BlockSpec(memory_space=pltpu.VMEM)
    return pl.pallas_call(
        functools.partial(reorder_kernel, sizes),
        out_shape=jax.ShapeDtypeStruct(shape, BF),
        in_specs=[vmem],
        out_specs=vmem,
        compiler_params=pltpu.CompilerParams(vmem_limit_bytes=16 << 20),
        cost_estimate=pl.CostEstimate(flops=1 << 29, bytes_accessed=2 << 20, transcendentals=0),
        name="reorder",
    )(rows)


def other_half(block):
    n = lax.axis_size("zl")
    spot = lambda h, z: z * 2 + h
    mirror = [(spot(h, z), spot(1 - h, n - 1 - z)) for h in (0, 1) for z in range(n)]
    return lax.ppermute(block, ("zl", "h"), mirror)


def on_device(
    rollout,
    agent_gain,
    time_gain,
    inner_gain,
    agent_pair,
    agent_value,
    agent_out,
    time_pair,
    time_value,
    time_out,
    expand_weight,
    reduce_weight,
    episode_start,
):
    steps_here, agents_here, width = rollout.shape
    core, high = lax.axis_index("c"), lax.axis_index("h")
    n_grp, n_core = lax.axis_size(GRP), lax.axis_size("c")

    half = expand_weight.shape[1] // 2
    up = lax.dynamic_slice_in_dim(expand_weight, core * half, half, 1)
    down = lax.dynamic_slice_in_dim(reduce_weight.T, core * half, half, 1)
    mine = jnp.stack([up, down])
    other = other_half(mine)

    rows = lax.all_to_all(rollout, GRP, split_axis=0, concat_axis=0, tiled=True)
    rows = rows.reshape(n_grp * agents_here, width)
    pair = jnp.where(
        high == 0, jnp.concatenate([mine, other], 1), jnp.concatenate([other, mine], 1)
    )
    rows, pair = lax.optimization_barrier((rows, pair))
    weights = lax.all_gather(pair[None], ("c", "x", "y"), axis=0, tiled=True)
    weights = weights.reshape(n_core, -1, 2, pair.shape[1], half)

    n_dev = lax.axis_size(DEV)
    agents_own = episode_start.shape[0]
    steps = n_dev * steps_here
    n_high = lax.axis_size("h")
    n_flat = n_dev // n_high
    normed = rms_scale(rows, agent_gain)
    queries = split_heads(linear(normed, agent_pair[0]).astype(BF))
    keys = split_heads(linear(normed, agent_pair[1]).astype(BF))
    values = split_heads(linear(normed, agent_value).astype(BF))
    context = attend(queries, keys, values)
    after_agents = (rows.astype(F32) + linear(context, agent_out)).astype(BF)

    pieces = after_agents.reshape(n_grp, n_flat, n_high, agents_own, width)
    pieces = jnp.transpose(pieces, (2, 1, 0, 3, 4)).reshape(steps, agents_own, width)
    series = lax.all_to_all(pieces, TURNED + GRP, split_axis=0, concat_axis=0, tiled=True)
    series = jnp.swapaxes(series, 0, 1)
    sizes = (n_flat, n_high, steps_here)
    after_time = time_block(
        series, sizes, episode_start, time_gain, time_pair, time_value, time_out
    )
    shape = (n_dev, agents_own, steps_here, width)
    result = ff_block(after_time, inner_gain, weights, shape)
    result = lax.all_to_all(result, TURNED, split_axis=0, concat_axis=0, tiled=True)
    return reorder((n_flat, n_high, agents_own, steps_here), result, rollout.shape)


def solution(mesh):
    fine = Mesh(mesh.devices.reshape(4, 2, 4, 4, 2), ("zl", "c", "x", "y", "h"))
    return jax.shard_map(
        on_device,
        mesh=fine,
        in_specs=(
            P(DEV, GRP, None),
            P(),
            P(),
            P(),
            P(),
            P(),
            P(),
            P(),
            P(),
            P(),
            P(DEV, None),
            P(None, DEV),
            P(GRP + DEV),
        ),
        out_specs=P(DEV, GRP, None),
        check_vma=False,
    )
```

```python
import functools

import jax
import jax.numpy as jnp
from jax import lax
from jax.experimental import pallas as pl
from jax.experimental.pallas import tpu as pltpu
from jax.sharding import Mesh, PartitionSpec as P

HDIM = 64
GRP = ("zl", "c")
DEV = ("x", "y", "h")
TURNED = ("h", "x", "y")
BF = jnp.bfloat16
F32 = jnp.float32


def rms_scale(row_block, gain_vec):
    widened = row_block.astype(F32)
    inverse = lax.rsqrt(jnp.mean(widened * widened, axis=-1, keepdims=True) + 1e-05)
    return (widened * inverse * gain_vec).astype(BF)


def linear(rows, weight):
    return jnp.dot(rows, weight, preferred_element_type=F32)


def split_heads(rows):
    return rows.reshape(rows.shape[0], -1, HDIM)


def attend(queries, keys, values):
    scores = jnp.einsum("ihd,jhd->hij", queries, keys, preferred_element_type=F32)
    scores = scores * HDIM ** (-0.5)
    exponent = jnp.exp(scores - jnp.max(scores, axis=-1, keepdims=True))
    total = jnp.sum(exponent, axis=-1)
    weighted = jnp.einsum("hij,jhd->ihd", exponent.astype(BF), values, preferred_element_type=F32)
    context = weighted / jnp.transpose(total)[..., None]
    return context.reshape(queries.shape[0], -1).astype(BF)


LOG2E = 1.4426950408889634


def rms_block(rows, gain):
    inverse = lax.rsqrt(jnp.mean(rows * rows, axis=-1, keepdims=True) + 1e-05)
    return (rows * inverse * gain).astype(BF)


def step_of(row, n_flat, n_high, block):
    low, flat = row & (block - 1), (row >> (block.bit_length() - 1)) & (n_flat - 1)
    high = row >> ((block * n_flat).bit_length() - 1)
    return (flat * n_high + high) * block + low


def time_kernel(sizes, start_ref, rows_ref, gain_ref, qk_ref, v_ref, o_ref, out_ref):
    agents, steps, width = rows_ref.shape
    later = step_of(lax.broadcasted_iota(jnp.int32, (steps, 1), 0), *sizes)
    earlier = step_of(lax.broadcasted_iota(jnp.int32, (1, steps), 1), *sizes)
    rows = jnp.concatenate([rows_ref[agent].astype(F32) for agent in range(agents)], 0)
    normed = rms_block(rows, gain_ref[...])
    queries = linear(normed, qk_ref[0]).astype(BF)
    keys = linear(normed, qk_ref[1]).astype(BF)
    values = linear(normed, v_ref[...]).astype(BF)
    context = []
    for agent in range(agents):
        begin = start_ref[agent]
        visible = (later >= earlier) & ((earlier >= begin) | (later < begin))
        own = slice(agent * steps, (agent + 1) * steps)
        parts = []
        for h in range(queries.shape[1] // HDIM):
            part = slice(h * HDIM, (h + 1) * HDIM)
            scores = lax.dot_general(
                queries[own, part], keys[own, part], (((1,), (1,)), ((), ())), preferred_element_type=F32
            )
            scores = jnp.where(visible, scores, -jnp.inf)
            top = jnp.max(scores, axis=-1, keepdims=True)
            exponent = jnp.exp2((scores - top) * (LOG2E * HDIM ** (-0.5)))
            total = jnp.sum(exponent, axis=-1, keepdims=True)
            weighted = linear(exponent.astype(BF), values[own, part])
            parts.append((weighted / total).astype(BF))
        context.append(jnp.concatenate(parts, 1))
    result = (rows + linear(jnp.concatenate(context, 0), o_ref[...])).astype(BF)
    for agent in range(agents):
        out_ref[agent] = result[agent * steps : (agent + 1) * steps]


def time_block(series, sizes, starts, gain, pair, value, out):
    agents, steps, width = series.shape
    vmem = pl.BlockSpec(memory_space=pltpu.VMEM)
    return pl.pallas_call(
        functools.partial(time_kernel, sizes),
        out_shape=jax.ShapeDtypeStruct(series.shape, BF),
        in_specs=[pl.BlockSpec(memory_space=pltpu.SMEM)] + [vmem] * 5,
        out_specs=vmem,
        compiler_params=pltpu.CompilerParams(vmem_limit_bytes=28 << 20),
        cost_estimate=pl.CostEstimate(flops=3 << 30, bytes_accessed=6 << 20, transcendentals=1 << 20),
        name="time_attention",
    )(starts, series, gain[None, :], pair, value, out)


def gelu(x):
    inner = 0.7978845608028654 * (x + 0.044715 * (x * x * x))
    return (0.5 * x) * (1.0 + jnp.tanh(inner))


def ff_kernel(which_ref, rows_ref, gain_ref, weights_ref, out_ref, held, arrived):
    halves, shards, _, depth, half = weights_ref.shape
    width, size = shards * depth, half // 2
    parts = [(i, j) for i in range(halves) for j in range(half // size)]

    def fetch(n, which):
        i, j = parts[n]
        source = weights_ref.at[i, :, which, :, pl.ds(j * size, size)]
        return pltpu.make_async_copy(source, held.at[n, which], arrived.at[n, which])

    fetch(0, 0).start()
    fetch(0, 1).start()
    count = rows_ref.shape[1] // 2
    here = pl.ds(pl.multiple_of(which_ref[0] * count, count), count)
    total = jnp.concatenate([rows_ref[a, here].astype(F32) for a in range(rows_ref.shape[0])], 0)
    inner = rms_block(total, gain_ref[...])
    for n in range(len(parts)):
        fetch(n, 0).wait()
        if n + 1 < len(parts):
            fetch(n + 1, 0).start()
            fetch(n + 1, 1).start()
        hidden = gelu(linear(inner, held[n, 0].reshape(width, size))).astype(BF)
        fetch(n, 1).wait()
        total = total + lax.dot_general(
            hidden,
            held[n, 1].reshape(width, size),
            (((1,), (1,)), ((), ())),
            preferred_element_type=F32,
        )
    blocks, agents, block, _ = out_ref.shape
    for agent in range(agents):
        part = total[agent * blocks * block : (agent + 1) * blocks * block]
        out_ref[:, agent] = part.reshape(blocks, block, width).astype(BF)


def ff_block(rows, gain, weights, which, shape):
    halves, shards, _, depth, half = weights.shape
    vmem = pl.BlockSpec(memory_space=pltpu.VMEM)
    return pl.pallas_call(
        ff_kernel,
        out_shape=jax.ShapeDtypeStruct(shape, BF),
        in_specs=[pl.BlockSpec(memory_space=pltpu.SMEM), vmem, vmem, pl.BlockSpec(memory_space=pltpu.HBM)],
        out_specs=vmem,
        scratch_shapes=[
            pltpu.VMEM((2 * halves, 2, shards, depth, half // 2), BF),
            pltpu.SemaphoreType.DMA((2 * halves, 2)),
        ],
        compiler_params=pltpu.CompilerParams(vmem_limit_bytes=50 << 20),
        cost_estimate=pl.CostEstimate(flops=4 << 30, bytes_accessed=10 << 20, transcendentals=1 << 20),
        name="feed_forward",
    )(which.reshape(1), rows, gain[None, :], weights)


def pick(places, rows):
    count = rows.shape[0]
    spot = lax.broadcasted_iota(jnp.int32, (places.shape[0], count), 1)
    return linear(jnp.where(spot == places, 1.0, 0.0).astype(BF), rows)


def reorder_kernel(sizes, high_ref, own_ref, other_ref, out_ref):
    n_flat, n_high, own, steps = sizes
    to = lax.broadcasted_iota(jnp.int32, (2 * own_ref.size // own_ref.shape[-1], 1), 0)
    bits = lambda n: n.bit_length() - 1
    agent, to = to & (own - 1), to >> bits(own)
    high, to = to & (n_high - 1), to >> bits(n_high)
    flat, step = to & (n_flat - 1), to >> bits(n_flat)
    place = (((high ^ high_ref[0]) * n_flat + flat) * own + agent) * steps + step
    width = own_ref.shape[-1]
    parts = [ref[...].astype(F32).reshape(-1, width) for ref in (own_ref, other_ref)]
    rows = jnp.concatenate(parts, 0).astype(BF)
    out_ref[...] = pick(place, rows).reshape(out_ref.shape).astype(BF)


def reorder(sizes, high, own, other, shape):
    vmem = pl.BlockSpec(memory_space=pltpu.VMEM)
    return pl.pallas_call(
        functools.partial(reorder_kernel, sizes),
        out_shape=jax.ShapeDtypeStruct(shape, BF),
        in_specs=[pl.BlockSpec(memory_space=pltpu.SMEM), vmem, vmem],
        out_specs=vmem,
        compiler_params=pltpu.CompilerParams(vmem_limit_bytes=16 << 20),
        cost_estimate=pl.CostEstimate(flops=1 << 29, bytes_accessed=2 << 20, transcendentals=0),
        name="reorder",
    )(high.reshape(1), own, other)


def other_half(block):
    n = lax.axis_size("zl")
    spot = lambda h, z: z * 2 + h
    mirror = [(spot(h, z), spot(1 - h, n - 1 - z)) for h in (0, 1) for z in range(n)]
    return lax.ppermute(block, ("zl", "h"), mirror)


def on_device(
    rollout,
    agent_gain,
    time_gain,
    inner_gain,
    agent_pair,
    agent_value,
    agent_out,
    time_pair,
    time_value,
    time_out,
    expand_weight,
    reduce_weight,
    episode_start,
):
    steps_here, agents_here, width = rollout.shape
    core, high = lax.axis_index("c"), lax.axis_index("h")
    n_grp, n_core = lax.axis_size(GRP), lax.axis_size("c")

    half = expand_weight.shape[1] // 2
    up = lax.dynamic_slice_in_dim(expand_weight, core * half, half, 1)
    down = lax.dynamic_slice_in_dim(reduce_weight.T, core * half, half, 1)
    mine = jnp.stack([up, down])
    other = other_half(mine)

    rows = lax.all_to_all(rollout, GRP, split_axis=0, concat_axis=0, tiled=True)
    rows = rows.reshape(n_grp * agents_here, width)
    pair = jnp.where(
        high == 0, jnp.concatenate([mine, other], 1), jnp.concatenate([other, mine], 1)
    )
    rows, pair = lax.optimization_barrier((rows, pair))
    weights = lax.all_gather(pair[None], ("c", "x", "y"), axis=0, tiled=True)
    weights = weights.reshape(n_core, -1, 2, pair.shape[1], half)

    n_dev = lax.axis_size(DEV)
    agents_own = episode_start.shape[0]
    steps = n_dev * steps_here
    n_high = lax.axis_size("h")
    n_flat = n_dev // n_high
    normed = rms_scale(rows, agent_gain)
    queries = split_heads(linear(normed, agent_pair[0]).astype(BF))
    keys = split_heads(linear(normed, agent_pair[1]).astype(BF))
    values = split_heads(linear(normed, agent_value).astype(BF))
    context = attend(queries, keys, values)
    after_agents = (rows.astype(F32) + linear(context, agent_out)).astype(BF)

    pieces = after_agents.reshape(n_grp, n_flat, n_high, agents_own, width)
    pieces = jnp.transpose(pieces, (2, 1, 0, 3, 4)).reshape(steps, agents_own, width)
    series = lax.all_to_all(pieces, TURNED + GRP, split_axis=0, concat_axis=0, tiled=True)
    series = jnp.swapaxes(series, 0, 1)
    sizes = (n_flat, n_high, steps_here)
    after_time = time_block(
        series, sizes, episode_start, time_gain, time_pair, time_value, time_out
    )
    shape = (n_flat, agents_own, steps_here, width)
    away = ff_block(after_time, inner_gain, weights, 1 - high, shape)
    away = lax.ppermute(away, "h", [(0, 1), (1, 0)])
    own = ff_block(after_time, inner_gain, weights, high, shape)
    own = lax.all_to_all(own, ("x", "y"), split_axis=0, concat_axis=0, tiled=True)
    away = lax.all_to_all(away, ("x", "y"), split_axis=0, concat_axis=0, tiled=True)
    return reorder((n_flat, n_high, agents_own, steps_here), high, own, away, rollout.shape)


def solution(mesh):
    fine = Mesh(mesh.devices.reshape(4, 2, 4, 4, 2), ("zl", "c", "x", "y", "h"))
    return jax.shard_map(
        on_device,
        mesh=fine,
        in_specs=(
            P(DEV, GRP, None),
            P(),
            P(),
            P(),
            P(),
            P(),
            P(),
            P(),
            P(),
            P(),
            P(DEV, None),
            P(None, DEV),
            P(GRP + DEV),
        ),
        out_specs=P(DEV, GRP, None),
        check_vma=False,
    )
```
